256 devices in a mesh: ctx: 32 (over y, z_lo, x), exp: 8 (over z_hi, core).
Axes of the slice: x: 4, y: 4, z: 8 (z_hi: 4, z_lo: 2; z = z_hi * 2 + z_lo), core: 2. Of those that a mesh axis runs over, the one named last changes fastest.
Arguments:
- lin_query: bfloat16 [4096, 8192], P('ctx', 'exp'), may hold values from -5 to 5
- lin_key: bfloat16 [4096, 8192], P('ctx', 'exp'), may hold values from -5 to 5
- lin_value: bfloat16 [4096, 8192], P('ctx', 'exp'), may hold values from -5 to 5
- log_decay: float32 [4096, 64], P('ctx', 'exp'), may hold values from -1.5 to 0
- lin_gain: float32 [8192], P('exp'), may hold values from 0.25 to 1.75
- moe_input: bfloat16 [1536, 6144], P(('ctx', 'exp')), may hold values from -6 to 6
- routes: int32 [1536, 2], P(('ctx', 'exp')), may hold values from 0 to 7, all different within a row; in each aligned block of 6 rows (0 to 5, 6 to 11, ...) at most 2 rows name the same one
- route_weight: float32 [1536, 2], P(('ctx', 'exp')), may hold values from 0.2 to 1
- gate_weight: bfloat16 [8, 6144, 9216], P('exp', None, 'ctx'), may hold values from -0.078125 to 0.078125
- up_weight: bfloat16 [8, 6144, 9216], P('exp', None, 'ctx'), may hold values from -0.078125 to 0.078125
- down_weight: bfloat16 [8, 9216, 6144], P('exp', 'ctx'), may hold values from -0.0625 to 0.0625
- soft_query: bfloat16 [4096, 8192], P('ctx', 'exp'), may hold values from -5 to 5
- soft_kv: bfloat16 [4096, 8, 2, 128], P('ctx', 'exp'), may hold values from -5 to 5
Outputs:
- lin_out: bfloat16 [4096, 8192], P('ctx', 'exp')
- moe_out: bfloat16 [1536, 6144], P(('ctx', 'exp'))
- soft_out: bfloat16 [4096, 8192], P('ctx', 'exp')
The draws below stay inside these ranges and needn't reach their ends.
Inputs may be any that keep to these rules, and one draw needn't show every extreme that they name: `routes`: within the rows of one device (6 rows) each expert is named by at most 2 of them; the 2 experts of a row differ.
All inputs are finite; a program needn't handle non-finite values.
Results may differ from the reference program's by a relative error of at most 0.009.
Values may be sent and summed in bfloat16 or wider, within the bound.
A program may use at most 128 MiB of HBM per device.

```python
import math
import jax
import jax.numpy as jnp
import numpy as np
from jax import lax

D = 6144
HEAD_TOTAL = 64
HEAD = 128
KV_HEADS = 8
FF = 9216
EXPERTS = 8
TOP = 2
SEQ_DEV = 128
MOE_DEV = 6
CAP = 2
CONTEXT_LENGTH = 4096
MOE_TOKENS = 1536


def draw_log_decay(key, part):
    random_subkeys = jax.random.split(key, 6)
    fast_cut = 5
    fast_head = jax.random.randint(random_subkeys[0], (HEAD_TOTAL,), 0, 10) < fast_cut
    fast_rate = jax.random.uniform(random_subkeys[1], (HEAD_TOTAL,), jnp.float32, 0.05, 0.1)
    slow_rate = jax.random.uniform(random_subkeys[2], (HEAD_TOTAL,), jnp.float32, 0.1, 0.4) / CONTEXT_LENGTH
    head_rate = jnp.where(fast_head, fast_rate, slow_rate)
    region_span = max(CONTEXT_LENGTH // 16, 1)
    token_positions = jnp.arange(CONTEXT_LENGTH)
    region = jnp.minimum(token_positions // region_span, 15)
    region_factor = jnp.exp(jax.random.uniform(random_subkeys[3], (16,), jnp.float32, -0.7, 0.7))
    step_fraction = region_factor[region][:, None] * head_rate[None, :]
    spike_locations = jax.random.randint(random_subkeys[4], (2,), 0, CONTEXT_LENGTH)
    spike_losses = jnp.log(jax.random.uniform(random_subkeys[5], (2, HEAD_TOTAL), jnp.float32, 0.55, 0.8))
    spike_events = jnp.zeros((CONTEXT_LENGTH, HEAD_TOTAL), jnp.float32)
    for item_count in range(2):
        spike_events = spike_events + jnp.where((token_positions == spike_locations[item_count])[:, None], spike_losses[item_count][None, :], 0.0)
    return (spike_events - step_fraction).astype(jnp.float32)


def draw_soft_query(key, part):
    base_key = jax.random.fold_in(key, 1)
    values = jnp.clip(jax.random.normal(base_key, (CONTEXT_LENGTH, HEAD_TOTAL * HEAD), jnp.float32), -4.0, 4.0)
    return values.astype(jnp.bfloat16)


def draw_soft_kv(key, part):
    base_key = jax.random.fold_in(key, 2)
    values = jnp.clip(jax.random.normal(base_key, (CONTEXT_LENGTH, KV_HEADS, 2, HEAD), jnp.float32), -4.0, 4.0)
    return values.astype(jnp.bfloat16)


def steps_of(rng, shape, cuts, low, top_value):
    level, own = 1.0, jax.random.fold_in(rng, 6)
    for dim, blocks in cuts:
        heights = jnp.exp(jax.random.uniform(jax.random.fold_in(own, dim), (blocks,), jnp.float32, low / len(cuts), top_value / len(cuts)))
        level = level * jnp.repeat(heights, shape[dim] // blocks).reshape([-1 if axis == dim else 1 for axis in range(len(shape))])
    return level


def shared_out(rng, own, number, rows, count, top, most, slope):
    order = jax.random.permutation(rng, count)
    packed, ordinary = portions_of(count, rows * top, most, slope, True), portions_of(count, rows * top, most, slope, False)
    places = jnp.arange(count)

    def named(tallies, offset_by):
        used = int((tallies > 0).sum())
        fixed = max(1, used // 4)
        passed = fixed + (places - fixed + offset_by * (used - fixed)) % max(1, count - fixed)
        return jnp.zeros((count,), jnp.int32).at[order[jnp.where(places < fixed, places, passed)]].set(jnp.asarray(tallies, jnp.int32))

    tallies = jnp.where(number % 4 == 0, named(packed, number // 4), named(ordinary, number - number // 4 - 1))
    mixed = jax.random.permutation(jax.random.fold_in(own, 3), count)
    donor, taker = mixed[0:count // 2 * 2:2], mixed[1:count // 2 * 2:2]
    margin = jnp.minimum(tallies[donor] - 1, most - tallies[taker]) // 2
    margin = jnp.where((donor == order[0]) | (taker == order[0]) | (tallies[taker] == 0), 0, jnp.maximum(margin, 0))
    passed = jax.random.randint(jax.random.fold_in(own, 4), (count // 2,), 0, 1 << 20) % (margin + 1)
    tallies = tallies.at[donor].add(-passed).at[taker].add(passed)
    members = jnp.searchsorted(jnp.cumsum(tallies), jnp.arange(rows * top), side="right").astype(jnp.int32)
    grid = members.reshape(top, rows).T
    grid = grid[jax.random.permutation(jax.random.fold_in(own, 1), rows)]
    offset_by = jax.random.randint(jax.random.fold_in(own, 2), (rows, 1), 0, top)
    return jnp.take_along_axis(grid, (jnp.arange(top)[None, :] + offset_by) % top, axis=1)


def portions_of(amount, total, limit, lean, full):
    weights = [(1 << 20) // math.isqrt(standing ** lean) + 1 for standing in range(1, amount + 1)]
    largest = limit if full else min(limit, max(-(-total // amount), total * weights[0] // sum(weights)))
    least = 1 if total - largest >= amount - 1 else 0
    holding, rest = [largest] + [least] * (amount - 1), total - largest - least * (amount - 1)
    while rest > 0:
        candidates = [i for i in range(1, amount) if holding[i] < largest] or [i for i in range(1, amount) if holding[i] < limit]
        whole, left = sum([weights[i] for i in candidates]), rest
        for i in candidates:
            addition = min(limit - holding[i], max(1, left * weights[i] // whole), rest)
            holding[i] = holding[i] + addition
            rest = rest - addition
    return np.array(holding)


def gaussian(rng, shape, scale, bound, cuts=(), held_as=jnp.bfloat16):
    drawn = scale * jax.random.normal(rng, shape, jnp.float32)
    if cuts:
        drawn = drawn * steps_of(rng, shape, cuts, -0.22, 0.18)
    return jnp.clip(drawn, -bound, bound).astype(held_as)


def setup_inputs(seed: int = 0) -> dict:
    key_list = jax.random.split(jax.random.key(seed), 14)
    lin_query = gaussian(key_list[0], (CONTEXT_LENGTH, HEAD_TOTAL * HEAD), 1.0, 5.0, ((0, 32), (1, 8)))
    lin_key = gaussian(key_list[1], (CONTEXT_LENGTH, HEAD_TOTAL * HEAD), 1.0, 5.0, ((0, 32), (1, 8)))
    lin_value = gaussian(key_list[2], (CONTEXT_LENGTH, HEAD_TOTAL * HEAD), 1.0, 5.0, ((0, 32), (1, 8)))
    log_decay = draw_log_decay(jax.random.fold_in(key_list[13], 71), 0)
    lin_gain = jnp.clip(1.0 + 0.15 * jax.random.normal(key_list[4], (HEAD_TOTAL * HEAD,), jnp.float32), 0.25, 1.75)
    moe_input = gaussian(key_list[5], (MOE_TOKENS, D), 1.0, 6.0, ((0, 256),))
    routes_keys = jax.random.split(jax.random.fold_in(key_list[6], 1), MOE_TOKENS // MOE_DEV)
    routes_turns = jax.random.permutation(jax.random.fold_in(key_list[6], 3), MOE_TOKENS // MOE_DEV)
    routes = jax.vmap(lambda own, number: shared_out(jax.random.fold_in(key_list[6], 2), own, number, MOE_DEV, EXPERTS, TOP, CAP, 1))(routes_keys, routes_turns).reshape((MOE_TOKENS, TOP))
    route_weight = jnp.clip(0.2 + 0.8 * jax.random.uniform(key_list[7], (MOE_TOKENS, TOP), jnp.float32) ** steps_of(key_list[7], (MOE_TOKENS, TOP), ((0, 256),), -0.2, 0.2), 0.2, 1.0)
    gate_weight = gaussian(key_list[8], (EXPERTS, D, FF), D ** -0.5, 0.078125, ((0, 8), (2, 32)))
    up_weight = gaussian(key_list[9], (EXPERTS, D, FF), D ** -0.5, 0.078125, ((0, 8), (2, 32)))
    down_weight = gaussian(key_list[10], (EXPERTS, FF, D), FF ** -0.5, 0.0625, ((0, 8), (1, 32)))
    soft_query = draw_soft_query(jax.random.fold_in(key_list[13], 71), 0)
    soft_kv = draw_soft_kv(jax.random.fold_in(key_list[13], 71), 0)
    return {"lin_query": lin_query, "lin_key": lin_key, "lin_value": lin_value, "log_decay": log_decay, "lin_gain": lin_gain, "moe_input": moe_input, "routes": routes, "route_weight": route_weight, "gate_weight": gate_weight, "up_weight": up_weight, "down_weight": down_weight, "soft_query": soft_query, "soft_kv": soft_kv}


def lightning_ref(lin_query, lin_key, lin_value, log_decay, lin_gain):
    block_count = CONTEXT_LENGTH // SEQ_DEV
    score_scale = 1.0 / math.sqrt(HEAD)
    query_blocks = lin_query.reshape(block_count, SEQ_DEV, HEAD_TOTAL, HEAD)
    key_blocks = lin_key.reshape(block_count, SEQ_DEV, HEAD_TOTAL, HEAD)
    value_blocks = lin_value.reshape(block_count, SEQ_DEV, HEAD_TOTAL, HEAD)
    decay_blocks = log_decay.reshape(block_count, SEQ_DEV, HEAD_TOTAL)
    causal = jnp.tril(jnp.ones((SEQ_DEV, SEQ_DEV), dtype=jnp.bool_))

    def block_step(running_state, inputs):
        query_part, key_part, value_part, decay_part = inputs
        query_f = query_part.astype(jnp.float32)
        key_f = key_part.astype(jnp.float32)
        value_f = value_part.astype(jnp.float32)
        cumulative = jnp.cumsum(decay_part, axis=0)
        scores = jnp.einsum('thd,jhd->htj', query_f, key_f, precision=lax.Precision.HIGHEST) * score_scale
        spread = cumulative.T[:, :, None] - cumulative.T[:, None, :]
        decays = jnp.where(causal[None], jnp.exp(jnp.where(causal[None], spread, 0.0)), 0.0)
        within = jnp.einsum('htj,jhd->thd', scores * decays, value_f, precision=lax.Precision.HIGHEST)
        carried = jnp.exp(cumulative)[:, :, None] * jnp.einsum('thd,hde->the', query_f, running_state, precision=lax.Precision.HIGHEST) * score_scale
        tail_decay = jnp.exp(cumulative[-1][None, :] - cumulative)
        local_state = jnp.einsum('th,thd,the->hde', tail_decay, key_f, value_f, precision=lax.Precision.HIGHEST)
        next_state = jnp.exp(cumulative[-1])[:, None, None] * running_state + local_state
        return (next_state, within + carried)
    start_state = jnp.zeros((HEAD_TOTAL, HEAD, HEAD), jnp.float32)
    final_state, combined = lax.scan(block_step, start_state, (query_blocks, key_blocks, value_blocks, decay_blocks))
    combined = combined.reshape(CONTEXT_LENGTH, HEAD_TOTAL, HEAD)
    root_mean = jnp.sqrt(lax.optimization_barrier(jnp.mean(combined * combined, axis=-1, keepdims=True)) + 1e-06)
    normed = combined / root_mean * lin_gain.reshape(HEAD_TOTAL, HEAD)
    return normed.reshape(CONTEXT_LENGTH, HEAD_TOTAL * HEAD).astype(jnp.bfloat16)

def experts_ref(moe_input, routes, route_weight, gate_weight, up_weight, down_weight):
    block_count = MOE_TOKENS // MOE_DEV
    pair_count = MOE_DEV * TOP
    flat_ids = routes.reshape(block_count, pair_count)
    same_expert = flat_ids[:, :, None] == flat_ids[:, None, :]
    pair_order = jnp.arange(pair_count, dtype=jnp.int32)
    earlier_pair = pair_order[None, :] < pair_order[:, None]
    slot_rank = lax.optimization_barrier(jnp.sum(jnp.logical_and(same_expert, earlier_pair[None]), axis=2)).astype(jnp.int32)
    block_ids = jnp.arange(block_count, dtype=jnp.int32)[:, None]
    row_index = (block_ids * CAP + slot_rank).astype(jnp.int32)
    pair_rows = jnp.repeat(moe_input, TOP, axis=0).reshape(block_count, pair_count, D)
    buffer = jnp.zeros((EXPERTS, block_count * CAP, D), jnp.bfloat16).at[flat_ids, row_index].set(pair_rows)

    def expert(inputs):
        tokens_in, gate_w, up_w, down_w = inputs
        gate_part = jnp.dot(tokens_in, gate_w, preferred_element_type=jnp.float32)
        up_part = jnp.dot(tokens_in, up_w, preferred_element_type=jnp.float32)
        hidden = (jax.nn.silu(gate_part) * up_part).astype(jnp.bfloat16)
        return jnp.dot(hidden, down_w, preferred_element_type=jnp.float32).astype(jnp.bfloat16)
    results = lax.map(expert, (buffer, gate_weight, up_weight, down_weight))
    pair_out = results[flat_ids, row_index].reshape(MOE_TOKENS, TOP, D).astype(jnp.float32)
    mixed = lax.optimization_barrier(jnp.sum(pair_out * route_weight[:, :, None], axis=1))
    return mixed.astype(jnp.bfloat16)

def softmax_ref(soft_query, soft_kv):
    group = HEAD_TOTAL // KV_HEADS
    score_scale = 1.0 / math.sqrt(HEAD)
    queries = soft_query.reshape(CONTEXT_LENGTH, HEAD_TOTAL, HEAD).transpose(1, 0, 2)
    keys_all = jnp.repeat(soft_kv[:, :, 0, :].transpose(1, 0, 2), group, axis=0)
    values_all = jnp.repeat(soft_kv[:, :, 1, :].transpose(1, 0, 2), group, axis=0)
    causal = jnp.tril(jnp.ones((CONTEXT_LENGTH, CONTEXT_LENGTH), dtype=jnp.bool_))

    def one_head(inputs):
        query_head, key_head, value_head = inputs
        scores = jnp.dot(query_head, key_head.T, preferred_element_type=jnp.float32) * score_scale
        scores = jnp.where(causal, scores, -jnp.inf)
        weights = jax.nn.softmax(scores, axis=-1).astype(jnp.bfloat16)
        return jnp.dot(weights, value_head, preferred_element_type=jnp.float32).astype(jnp.bfloat16)
    outputs = lax.map(one_head, (queries, keys_all, values_all))
    return outputs.transpose(1, 0, 2).reshape(CONTEXT_LENGTH, HEAD_TOTAL * HEAD)

def reference(lin_query, lin_key, lin_value, log_decay, lin_gain, moe_input, routes, route_weight, gate_weight, up_weight, down_weight, soft_query, soft_kv):
    lin_out = lightning_ref(lin_query, lin_key, lin_value, log_decay, lin_gain)
    moe_out = experts_ref(moe_input, routes, route_weight, gate_weight, up_weight, down_weight)
    soft_out = softmax_ref(soft_query, soft_kv)
    return (lin_out, moe_out, soft_out)
```

```python
import math

import jax
import jax.numpy as jnp
from jax import lax
from jax.experimental import pallas as pl
from jax.experimental.pallas import tpu as pltpu
from jax.sharding import PartitionSpec as P

D = 6144
HEAD = 128
EXPERTS = 8
TOP = 2
CAP = 2
CTX = 32
SEQ = 128
HEADS = 8
FF = 288
ROWS = 16
SCALE = 1.0 / math.sqrt(HEAD)
F32, BF16 = jnp.float32, jnp.bfloat16
MESH = pl.DeviceIdType.MESH
DFS = (2, 1, -1, 0)


def dot(a, b, dims=((1,), (0,))):
    return lax.dot_general(a, b, (dims, ((), ())), preferred_element_type=F32)


def dot_split(a, b, dims=((1,), (0,))):
    high = a.astype(BF16)
    low = (a - high.astype(F32)).astype(BF16)
    return dot(high, b, dims) + dot(low, b, dims)


def kernel(
    slabs, kv_own, gate_hbm, up_hbm, down_hbm, lin_q, lin_k, lin_v, decay, decay_t, gain, soft_q,
    ret, lin_out, soft_out,
    kv, tok, part, s1r, s2r, f1r, f2r, zr, got, back, wide, gate, up, down, hidden,
    bias, cum, cum_t, state_out, state_in, prior_out, prior,
    w_sem, kv_send, kv_recv, tok_send, tok_recv, rs_send, s1_sem, s2_sem, f1_sem, f2_sem, z_sem,
    go_send, go_recv, back_send, back_recv, st_send, st_recv, pr_send, pr_recv,
):
    c, e = lax.axis_index("ctx"), lax.axis_index("exp")
    y, z, x, core = c // 8, (c // 4) % 2, c % 4, e % 2
    f, s = x + core * (y - x), y + core * (x - y)

    def rel(step):
        ds, df, dz = step
        return (s + ds + 4) % 4, (f + df + 4) % 4, (z + dz) % 2

    def ctx_of(step):
        ss, ff, zz = rel(step)
        return (ss + core * (ff - ss)) * 8 + zz * 4 + ff + core * (ss - ff)

    def index_of(step):
        ss, ff, zz = rel(step)
        return ss * 8 + ff * 2 + zz

    def rows_of(step, rows):
        return pl.ds(pl.multiple_of(index_of(step) * rows, rows), rows)

    barrier = pltpu.get_barrier_semaphore()

    @pl.loop(1, CTX)
    def _(k):
        pl.semaphore_signal(barrier, inc=1, device_id=((c + k) % CTX, e), device_id_type=MESH)

    @pl.loop(1, EXPERTS)
    def _(k):
        pl.semaphore_signal(barrier, inc=1, device_id=(c, (e + k) % EXPERTS), device_id_type=MESH)

    pl.semaphore_wait(barrier, CTX - 1 + EXPERTS - 1)

    weights = [
        pltpu.make_async_copy(src, dst, w_sem.at[i])
        for i, (src, dst) in enumerate(((gate_hbm, gate), (up_hbm, up), (down_hbm, down)))
    ]
    for copy in weights:
        copy.start()

    unfinished = []

    def push(src, dst, send_sem, recv_sem, to):
        copy = pltpu.make_async_remote_copy(
            src_ref=src, dst_ref=dst, send_sem=send_sem, recv_sem=recv_sem, device_id=to, device_id_type=MESH
        )
        copy.start()
        unfinished.append(copy)

    def landed(ref, recv_sem, spare_sem):
        pltpu.make_async_remote_copy(
            src_ref=ref, dst_ref=ref, send_sem=spare_sem, recv_sem=recv_sem,
            device_id=(ctx_of((0, 0, 1)), e), device_id_type=MESH,
        ).wait_recv()

    def gather(buf, rows, send_sems, recv_sems):
        used = [0]

        def send(step, to):
            where = rows_of(step, rows)
            push(buf.at[where], buf.at[where], send_sems.at[used[0]], recv_sems.at[index_of(step)], (ctx_of(to), e))
            used[0] += 1

        def sideways(step):
            send(step, (1, 0, 0))
            send(step, (-1, 0, 0))

        def own():
            send((0, 0, 0), (0, 0, 1))
            send((0, 0, 0), (0, 1, 0))
            send((0, 0, 0), (0, -1, 0))
            sideways((0, 0, 0))

        def arrive(*steps):
            for step in steps:
                ds, df, dz = step
                landed(buf.at[rows_of(step, rows)], recv_sems.at[index_of(step)], send_sems.at[0])
                if ds == 0:
                    if df == 0:
                        send(step, (0, 1, 0))
                        send(step, (0, -1, 0))
                    elif df == -1 and dz == 0:
                        send(step, (0, 1, 0))
                    elif df == 1 and dz == 1:
                        send(step, (0, -1, 0))
                    sideways(step)
                elif ds == -1 and dz == 0:
                    send(step, (1, 0, 0))
                elif ds == 1 and dz == 1:
                    send(step, (-1, 0, 0))

        return own, arrive

    kv_first, kv_arrive = gather(kv, SEQ, kv_send, kv_recv)
    tok_first, tok_arrive = gather(tok, ROWS, tok_send, tok_recv)

    @pl.loop(1, EXPERTS)
    def _(k):
        to = (e + k) % EXPERTS
        pltpu.make_async_remote_copy(
            src_ref=slabs.at[to], dst_ref=got.at[e], send_sem=go_send.at[to], recv_sem=go_recv.at[e],
            device_id=(c, to), device_id_type=MESH,
        ).start()

    kv[rows_of((0, 0, 0), SEQ), :] = kv_own[...]
    kv_first()

    row = lax.broadcasted_iota(jnp.int32, (SEQ, SEQ), 0)
    col = lax.broadcasted_iota(jnp.int32, (SEQ, SEQ), 1)
    lower = (col <= row).astype(BF16)

    def three(a):
        high = a.astype(BF16)
        mid = (a - high.astype(F32)).astype(BF16)
        low = (a - high.astype(F32) - mid.astype(F32)).astype(BF16)
        return high, mid, low

    cum[...] = sum(dot(lower, term) for term in three(decay[...]))
    cum_t[...] = sum(dot(term, lower, ((1,), (1,))) for term in three(decay_t[...]))
    last = cum[SEQ - 1 : SEQ, :]
    line = lax.broadcasted_iota(jnp.int32, (16, HEAD), 0)
    for h in range(HEADS):
        tail = jnp.exp(last[:, h : h + 1] - cum[:, h : h + 1])
        head = pl.ds(h * HEAD, HEAD)
        scaled = lin_k[:, head].astype(F32) * tail
        state = dot_split(scaled.T, lin_v[:, head])
        high, mid, low = (jnp.broadcast_to(t.astype(F32), (16, HEAD)) for t in three(last[:, h : h + 1]))
        logs = jnp.where(line == 0, high, jnp.where(line == 1, mid, jnp.where(line == 2, low, 0.0))).astype(BF16)
        for i in range(4):
            state_out[4 * h + i, 0:32, :] = state[32 * i : 32 * i + 32].astype(BF16)
            state_out[4 * h + i, 32:48, :] = logs

    @pl.loop(1, CTX)
    def _(k):
        to = (c + k) % CTX
        pltpu.make_async_remote_copy(
            src_ref=state_out.at[to], dst_ref=state_in.at[c], send_sem=st_send.at[to], recv_sem=st_recv.at[c],
            device_id=(to, e), device_id_type=MESH,
        ).start()

    state_in[c] = state_out[c]

    kv_arrive((0, 0, 1), (0, 1, 0), (0, -1, 0), (1, 0, 0), (-1, 0, 0))

    got[e] = slabs[e]

    @pl.loop(1, EXPERTS)
    def _(k):
        at = (e + k) % EXPERTS
        pltpu.make_async_remote_copy(
            src_ref=slabs.at[at], dst_ref=got.at[at], send_sem=go_send.at[at], recv_sem=go_recv.at[at],
            device_id=(c, at), device_id_type=MESH,
        ).wait()

    for i in range(EXPERTS):
        wide[2 * i : 2 * i + 2, :] = got[i].astype(F32)
    tok[rows_of((0, 0, 0), ROWS), :] = wide[...].astype(BF16)
    tok_first()

    kv_arrive((0, 1, 1), (0, -1, 1), (1, 0, 1), (-1, 0, 1), (0, 2, 0), (0, 2, 1))
    kv_arrive(*((ds, df, 0) for df in (1, -1) for ds in (1, -1)))
    tok_arrive((0, 0, 1), (0, 1, 0), (0, -1, 0), (1, 0, 0), (-1, 0, 0))
    kv_arrive(*((ds, df, 1) for df in (1, -1) for ds in (1, -1)))
    kv_arrive(*((ds, 2, dz) for dz in (0, 1) for ds in (1, -1)))
    kv_arrive(*((2, df, dz) for df in (0, 1, -1, 2) for dz in (0, 1)))
    tok_arrive((0, 1, 1), (0, -1, 1))

    @pl.loop(1, CTX)
    def _(k):
        at = (c + k) % CTX
        pltpu.make_async_remote_copy(
            src_ref=state_out.at[at], dst_ref=state_in.at[at], send_sem=st_send.at[at], recv_sem=st_recv.at[at],
            device_id=(at, e), device_id_type=MESH,
        ).wait()

    def hop(i, run):
        prior_out[i] = run.astype(BF16)
        logs = jnp.sum(state_in[i, 32:48, :].astype(F32), axis=0, keepdims=True)
        return jnp.exp(logs) * run + state_in[i, 0:32, :].astype(F32)

    lax.fori_loop(0, CTX, hop, jnp.zeros((32, HEAD), F32))

    @pl.loop(1, CTX)
    def _(k):
        to = (c + k) % CTX
        pltpu.make_async_remote_copy(
            src_ref=prior_out.at[to], dst_ref=prior.at[c], send_sem=pr_send.at[to], recv_sem=pr_recv.at[c],
            device_id=(to, e), device_id_type=MESH,
        ).start()

    prior[c] = prior_out[c]

    wide_col = lax.broadcasted_iota(jnp.int32, (8, CTX * SEQ), 1)
    blk = jnp.right_shift(wide_col, 7)
    b_s, b_f, b_z = jnp.right_shift(blk, 3), jnp.bitwise_and(jnp.right_shift(blk, 1), 3), jnp.bitwise_and(blk, 1)
    b_ctx = (b_s + core * (b_f - b_s)) * 8 + b_z * 4 + b_f + core * (b_s - b_f)
    place = b_ctx * SEQ + jnp.bitwise_and(wide_col, SEQ - 1)
    line8 = lax.broadcasted_iota(jnp.int32, (8, CTX * SEQ), 0)

    @pl.loop(0, SEQ // 8)
    def _(i):
        bias[pl.ds(pl.multiple_of(i * 8, 8), 8), :] = jnp.where(place <= c * SEQ + i * 8 + line8, 0.0, -1e30)

    def attend(first, count):
        @pl.loop(first, first + count)
        def _(h):
            head = pl.ds(pl.multiple_of(h * HEAD, HEAD), HEAD)
            scores = dot(soft_q[:, head], kv[:, 0:HEAD], ((1,), (1,))) * SCALE + bias[...]
            top = jnp.max(scores, axis=1, keepdims=True)
            probs = jnp.exp(scores - top)
            total = jnp.sum(probs, axis=1, keepdims=True)
            mixed = dot(probs.astype(BF16), kv[:, HEAD : 2 * HEAD])
            soft_out[:, head] = (mixed / total).astype(BF16)

    def finish_lightning(heads):
        for h in heads:
            head = pl.ds(h * HEAD, HEAD)
            here = cum[:, h : h + 1]
            spread = here - cum_t[h : h + 1, :]
            decays = jnp.where(col <= row, jnp.exp(jnp.where(col <= row, spread, 0.0)), 0.0)
            scores = dot(lin_q[:, head], lin_k[:, head], ((1,), (1,))) * SCALE
            within = dot_split(scores * decays, lin_v[:, head])
            before = prior[4 * h : 4 * h + 4].reshape(HEAD, HEAD)
            combined = within + jnp.exp(here) * dot(lin_q[:, head], before) * SCALE
            root = jnp.sqrt(jnp.mean(combined * combined, axis=1, keepdims=True) + 1e-06)
            lin_out[:, head] = (combined / root * gain[:, head]).astype(BF16)

    chunk = 1024

    def group(ds):
        return pl.ds(pl.multiple_of((s + ds + 4) % 4 * 8 * ROWS, 8 * ROWS), 8 * ROWS)

    def enter(ds):
        def add(k, sums):
            at = pl.ds(pl.multiple_of(k * chunk, chunk), chunk)
            tokens = tok[group(ds), at]
            return sums[0] + dot(tokens, gate[at, :]), sums[1] + dot(tokens, up[at, :])

        zero = jnp.zeros((8 * ROWS, FF), F32)
        a, b = lax.fori_loop(0, D // chunk, add, (zero, zero))
        hidden[group(ds), :] = (a / (1.0 + jnp.exp(-a)) * b).astype(BF16)

    def leave(ds):
        @pl.loop(0, D // chunk)
        def _(k):
            at = pl.ds(pl.multiple_of(k * chunk, chunk), chunk)
            part[group(ds), at] = dot(hidden[group(ds), :], down[:, at]).astype(BF16)

    attend(0, 1)
    tok_arrive((1, 0, 1), (-1, 0, 1), (0, 2, 0), (0, 2, 1))
    attend(1, 1)
    tok_arrive(*((ds, df, 0) for df in (1, -1) for ds in (1, -1)))
    attend(2, 1)
    attend(3, 1)
    tok_arrive(*((ds, df, 1) for df in (1, -1) for ds in (1, -1)))
    attend(4, 2)
    for copy in weights:
        copy.wait()
    enter(0)
    tok_arrive(*((ds, 2, dz) for dz in (0, 1) for ds in (1, -1)))
    attend(6, 2)
    enter(1)
    enter(-1)
    tok_arrive(*((2, df, dz) for df in (0, 1, -1, 2) for dz in (0, 1)))
    enter(2)

    rs_used = [0]

    def send_part(step, dst, sem, to):
        push(part.at[rows_of(step, ROWS)], dst, rs_send.at[rs_used[0]], sem, (ctx_of(to), e))
        rs_used[0] += 1

    def block(ref, i):
        return ref.at[pl.ds(i * ROWS, ROWS)]

    def add_in(step, *blocks):
        where = rows_of(step, ROWS)
        total = part[where, :].astype(F32)
        for b in blocks:
            total = total + b[...].astype(F32)
        part[where, :] = total.astype(BF16)

    leave(2)
    for i, df in enumerate(DFS):
        send_part((2, df, 0), block(s1r, 2 * i), s1_sem.at[2 * i], (-1, 0, 0))
        send_part((2, df, 1), block(s1r, 2 * i + 1), s1_sem.at[2 * i + 1], (1, 0, 0))
    leave(-1)
    for i, df in enumerate(DFS):
        send_part((-1, df, 1), block(s2r, 4 * i + 1), s2_sem.at[4 * i + 1], (-1, 0, 0))
    leave(1)
    for i, df in enumerate(DFS):
        send_part((1, df, 0), block(s2r, 4 * i + 2), s2_sem.at[4 * i + 2], (1, 0, 0))
    leave(0)

    @pl.loop(1, CTX)
    def _(k):
        at = (c + k) % CTX
        pltpu.make_async_remote_copy(
            src_ref=prior_out.at[at], dst_ref=prior.at[at], send_sem=pr_send.at[at], recv_sem=pr_recv.at[at],
            device_id=(at, e), device_id_type=MESH,
        ).wait()

    for i, df in enumerate(DFS):
        for k, step, to in ((0, (-1, df, 0), (-1, 0, 0)), (1, (1, df, 1), (1, 0, 0))):
            landed(block(s1r, 2 * i + k), s1_sem.at[2 * i + k], rs_send.at[0])
            add_in(step, block(s1r, 2 * i + k))
            slot = 4 * i + (0 if k == 0 else 3)
            send_part(step, block(s2r, slot), s2_sem.at[slot], to)
        finish_lightning((2 * i, 2 * i + 1))

    for i, df in enumerate(DFS):
        for slot in (1, 2, 0, 3):
            landed(block(s2r, 4 * i + slot), s2_sem.at[4 * i + slot], rs_send.at[0])
        add_in((0, df, 0), block(s2r, 4 * i), block(s2r, 4 * i + 2))
        add_in((0, df, 1), block(s2r, 4 * i + 1), block(s2r, 4 * i + 3))
        if df == 2:
            send_part((0, 2, 0), block(f1r, 0), f1_sem.at[0], (0, -1, 0))
            send_part((0, 2, 1), block(f1r, 1), f1_sem.at[1], (0, 1, 0))
        elif df == 1:
            send_part((0, 1, 0), block(f2r, 2), f2_sem.at[2], (0, 1, 0))
        elif df == -1:
            send_part((0, -1, 1), block(f2r, 1), f2_sem.at[1], (0, -1, 0))
            for k, step, to in ((0, (0, -1, 0), (0, -1, 0)), (1, (0, 1, 1), (0, 1, 0))):
                landed(block(f1r, k), f1_sem.at[k], rs_send.at[0])
                add_in(step, block(f1r, k))
                slot = 0 if k == 0 else 3
                send_part(step, block(f2r, slot), f2_sem.at[slot], to)

    landed(block(f2r, 1), f2_sem.at[1], rs_send.at[0])
    landed(block(f2r, 3), f2_sem.at[3], rs_send.at[0])
    add_in((0, 0, 1), block(f2r, 1), block(f2r, 3))
    send_part((0, 0, 1), zr, z_sem.at[0], (0, 0, 1))
    landed(block(f2r, 0), f2_sem.at[0], rs_send.at[0])
    landed(block(f2r, 2), f2_sem.at[2], rs_send.at[0])
    wide[...] = (
        part[rows_of((0, 0, 0), ROWS), :].astype(F32)
        + block(f2r, 0)[...].astype(F32)
        + block(f2r, 2)[...].astype(F32)
    )
    landed(zr, z_sem.at[0], rs_send.at[0])
    wide[...] = wide[...] + zr[...].astype(F32)

    for i in range(EXPERTS):
        back[i] = wide[2 * i : 2 * i + 2, :].astype(BF16)

    @pl.loop(1, EXPERTS)
    def _(k):
        to = (e + k) % EXPERTS
        pltpu.make_async_remote_copy(
            src_ref=back.at[to], dst_ref=ret.at[e], send_sem=back_send.at[to], recv_sem=back_recv.at[e],
            device_id=(c, to), device_id_type=MESH,
        ).start()

    ret[e] = back[e]

    @pl.loop(1, EXPERTS)
    def _(k):
        at = (e + k) % EXPERTS
        pltpu.make_async_remote_copy(
            src_ref=back.at[at], dst_ref=ret.at[at], send_sem=back_send.at[at], recv_sem=back_recv.at[at],
            device_id=(c, at), device_id_type=MESH,
        ).wait()

    for copy in unfinished:
        copy.wait_send()


def on_device(
    lin_query,
    lin_key,
    lin_value,
    log_decay,
    lin_gain,
    moe_input,
    routes,
    route_weight,
    gate_weight,
    up_weight,
    down_weight,
    soft_query,
    soft_kv,
):
    rows = moe_input.shape[0]
    pairs = rows * TOP
    flat = routes.reshape(pairs)
    order = jnp.arange(pairs, dtype=jnp.int32)
    rank = jnp.sum((flat[:, None] == flat[None, :]) & (order[None, :] < order[:, None]), axis=1)
    slot = (flat * CAP + rank).reshape(rows, TOP)
    chosen = slot[None] == jnp.arange(CAP * EXPERTS, dtype=jnp.int32)[:, None, None]
    pick = jnp.any(chosen, axis=2).astype(BF16)
    slabs = jnp.dot(pick, moe_input, preferred_element_type=F32).astype(BF16).reshape(EXPERTS, CAP, D)

    vmem, any_ = pl.BlockSpec(memory_space=pltpu.VMEM), pl.BlockSpec(memory_space=pl.ANY)
    dma = pltpu.SemaphoreType.DMA
    ret, lin_out, soft_out = pl.pallas_call(
        kernel,
        out_shape=(
            jax.ShapeDtypeStruct((EXPERTS, CAP, D), BF16),
            jax.ShapeDtypeStruct((SEQ, HEADS * HEAD), BF16),
            jax.ShapeDtypeStruct((SEQ, HEADS * HEAD), BF16),
        ),
        in_specs=[vmem, vmem, any_, any_, any_] + [vmem] * 7,
        out_specs=(vmem, vmem, vmem),
        scratch_shapes=[
            pltpu.VMEM((CTX * SEQ, 2 * HEAD), BF16),
            pltpu.VMEM((CTX * ROWS, D), BF16),
            pltpu.VMEM((CTX * ROWS, D), BF16),
            pltpu.VMEM((8 * ROWS, D), BF16),
            pltpu.VMEM((16 * ROWS, D), BF16),
            pltpu.VMEM((2 * ROWS, D), BF16),
            pltpu.VMEM((4 * ROWS, D), BF16),
            pltpu.VMEM((ROWS, D), BF16),
            pltpu.VMEM((EXPERTS, CAP, D), BF16),
            pltpu.VMEM((EXPERTS, CAP, D), BF16),
            pltpu.VMEM((ROWS, D), F32),
            pltpu.VMEM((D, FF), BF16),
            pltpu.VMEM((D, FF), BF16),
            pltpu.VMEM((FF, D), BF16),
            pltpu.VMEM((CTX * ROWS, FF), BF16),
            pltpu.VMEM((SEQ, CTX * SEQ), F32),
            pltpu.VMEM((SEQ, HEADS), F32),
            pltpu.VMEM((HEADS, SEQ), F32),
            pltpu.VMEM((CTX, 48, HEAD), BF16),
            pltpu.VMEM((CTX, 48, HEAD), BF16),
            pltpu.VMEM((CTX, 32, HEAD), BF16),
            pltpu.VMEM((CTX, 32, HEAD), BF16),
            dma((3,)),
            dma((31,)), dma((32,)), dma((31,)), dma((32,)), dma((31,)),
            dma((8,)), dma((16,)), dma((2,)), dma((4,)), dma((1,)),
            dma((EXPERTS,)), dma((EXPERTS,)), dma((EXPERTS,)), dma((EXPERTS,)),
            dma((CTX,)), dma((CTX,)), dma((CTX,)), dma((CTX,)),
        ],
        compiler_params=pltpu.CompilerParams(
            collective_id=0, has_side_effects=True, vmem_limit_bytes=58 * 2**20
        ),
    )(
        slabs,
        soft_kv.reshape(SEQ, 2 * HEAD),
        gate_weight.reshape(D, FF),
        up_weight.reshape(D, FF),
        down_weight.reshape(FF, D),
        lin_query,
        lin_key,
        lin_value,
        log_decay,
        log_decay.T,
        lin_gain.reshape(1, HEADS * HEAD),
        soft_query,
    )
    mix = jnp.sum(jnp.where(chosen, route_weight[None], 0.0), axis=2)
    moe_out = lax.dot_general(
        mix, ret.reshape(CAP * EXPERTS, D).astype(F32), (((0,), (0,)), ((), ())), precision=lax.Precision.HIGHEST
    ).astype(BF16)
    return (lin_out, moe_out, soft_out)


def solution(mesh):
    placed = (
        P("ctx", "exp"),
        P("ctx", "exp"),
        P("ctx", "exp"),
        P("ctx", "exp"),
        P("exp"),
        P(("ctx", "exp"), None),
        P(("ctx", "exp"), None),
        P(("ctx", "exp"), None),
        P("exp", None, "ctx"),
        P("exp", None, "ctx"),
        P("exp", "ctx", None),
        P("ctx", "exp"),
        P("ctx", "exp", None, None),
    )
    return jax.shard_map(
        on_device,
        mesh=mesh,
        in_specs=placed,
        out_specs=(P("ctx", "exp"), P(("ctx", "exp"), None), P("ctx", "exp")),
        check_vma=False,
    )
```

```python
import math

import jax
import jax.numpy as jnp
from jax import lax
from jax.experimental import pallas as pl
from jax.experimental.pallas import tpu as pltpu
from jax.sharding import PartitionSpec as P

D = 6144
HEAD = 128
EXPERTS = 8
TOP = 2
CAP = 2
CTX = 32
SEQ = 128
HEADS = 8
FF = 288
ROWS = 16
SCALE = 1.0 / math.sqrt(HEAD)
F32, BF16 = jnp.float32, jnp.bfloat16
MESH = pl.DeviceIdType.MESH
DFS = (2, 1, -1, 0)


def dot(a, b, dims=((1,), (0,))):
    return lax.dot_general(a, b, (dims, ((), ())), preferred_element_type=F32)


def dot_split(a, b, dims=((1,), (0,))):
    high = a.astype(BF16)
    low = (a - high.astype(F32)).astype(BF16)
    return dot(high, b, dims) + dot(low, b, dims)


def slots_of(routes):
    line = lax.broadcasted_iota(jnp.int32, (ROWS, 1), 0)
    expert, place = jnp.right_shift(line, 1), jnp.bitwise_and(line, 1)
    met = jnp.zeros((ROWS, 1), jnp.int32)
    found = []
    for r in range(6):
        named = (expert == routes[0, r]) | (expert == routes[1, r])
        found.append((expert, named & (met == place)))
        met = met + named.astype(jnp.int32)
    return found


def finish(routes, weights, ret, lin, soft, lin_out, moe_out, soft_out, wide):
    lin_out[...] = lin[...]
    soft_out[...] = soft[...]
    for i in range(EXPERTS):
        wide[2 * i : 2 * i + 2, :] = ret[i].astype(F32)
    for r, (expert, taken) in enumerate(slots_of(routes)):
        weight = jnp.where(expert == routes[0, r], weights[0, r], weights[1, r])
        mixed = jnp.sum(jnp.where(taken, weight, 0.0) * wide[...], axis=0, keepdims=True)
        moe_out[r : r + 1, :] = mixed.astype(BF16)


def kernel(
    routes, moe_in, kv_own, gate_hbm, up_hbm, down_hbm, lin_q, lin_k, lin_v, decay_t, gain, soft_q,
    ret, lin_out, soft_out,
    kv, tok, part, s1r, s2r, f1r, f2r, zr, slabs, got, back, wide, gate, up, down, hidden,
    bias, cum, cum_t, state_out, state_in, prior_out, prior,
    w_sem, kv_send, kv_recv, tok_send, tok_recv, rs_send, s1_sem, s2_sem, f1_sem, f2_sem, z_sem,
    go_send, go_recv, back_send, back_recv, st_send, st_recv, pr_send, pr_recv,
):
    c, e = lax.axis_index("ctx"), lax.axis_index("exp")
    y, z, x, core = c // 8, (c // 4) % 2, c % 4, e % 2
    f, s = x + core * (y - x), y + core * (x - y)

    def rel(step):
        ds, df, dz = step
        return (s + ds + 4) % 4, (f + df + 4) % 4, (z + dz) % 2

    def ctx_of(step):
        ss, ff, zz = rel(step)
        return (ss + core * (ff - ss)) * 8 + zz * 4 + ff + core * (ss - ff)

    def index_of(step):
        ss, ff, zz = rel(step)
        return ss * 8 + ff * 2 + zz

    def rows_of(step, rows):
        return pl.ds(pl.multiple_of(index_of(step) * rows, rows), rows)

    barrier = pltpu.get_barrier_semaphore()

    @pl.loop(1, CTX)
    def _(k):
        pl.semaphore_signal(barrier, inc=1, device_id=((c + k) % CTX, e), device_id_type=MESH)

    @pl.loop(1, EXPERTS)
    def _(k):
        pl.semaphore_signal(barrier, inc=1, device_id=(c, (e + k) % EXPERTS), device_id_type=MESH)

    pl.semaphore_wait(barrier, CTX - 1 + EXPERTS - 1)

    weights = [
        pltpu.make_async_copy(src, dst, w_sem.at[i])
        for i, (src, dst) in enumerate(((gate_hbm, gate), (up_hbm, up), (down_hbm, down)))
    ]
    for copy in weights:
        copy.start()

    unfinished = []

    def push(src, dst, send_sem, recv_sem, to):
        copy = pltpu.make_async_remote_copy(
            src_ref=src, dst_ref=dst, send_sem=send_sem, recv_sem=recv_sem, device_id=to, device_id_type=MESH
        )
        copy.start()
        unfinished.append(copy)

    def landed(ref, recv_sem, spare_sem):
        pltpu.make_async_remote_copy(
            src_ref=ref, dst_ref=ref, send_sem=spare_sem, recv_sem=recv_sem,
            device_id=(ctx_of((0, 0, 1)), e), device_id_type=MESH,
        ).wait_recv()

    def gather(buf, rows, send_sems, recv_sems):
        used = [0]

        def send(step, to):
            where = rows_of(step, rows)
            push(buf.at[where], buf.at[where], send_sems.at[used[0]], recv_sems.at[index_of(step)], (ctx_of(to), e))
            used[0] += 1

        def sideways(step):
            send(step, (1, 0, 0))
            send(step, (-1, 0, 0))

        def own():
            send((0, 0, 0), (0, 0, 1))
            send((0, 0, 0), (0, 1, 0))
            send((0, 0, 0), (0, -1, 0))
            sideways((0, 0, 0))

        def arrive(*steps):
            for step in steps:
                ds, df, dz = step
                landed(buf.at[rows_of(step, rows)], recv_sems.at[index_of(step)], send_sems.at[0])
                if ds == 0:
                    if df == 0:
                        send(step, (0, 1, 0))
                        send(step, (0, -1, 0))
                    elif df == -1 and dz == 0:
                        send(step, (0, 1, 0))
                    elif df == 1 and dz == 1:
                        send(step, (0, -1, 0))
                    sideways(step)
                elif ds == -1 and dz == 0:
                    send(step, (1, 0, 0))
                elif ds == 1 and dz == 1:
                    send(step, (-1, 0, 0))

        return own, arrive

    kv_first, kv_arrive = gather(kv, SEQ, kv_send, kv_recv)
    tok_first, tok_arrive = gather(tok, ROWS, tok_send, tok_recv)

    wide[...] = sum(
        taken.astype(F32) * moe_in[r : r + 1, :].astype(F32) for r, (_, taken) in enumerate(slots_of(routes))
    )
    for i in range(EXPERTS):
        slabs[i] = wide[2 * i : 2 * i + 2, :].astype(BF16)

    @pl.loop(1, EXPERTS)
    def _(k):
        to = (e + k) % EXPERTS
        pltpu.make_async_remote_copy(
            src_ref=slabs.at[to], dst_ref=got.at[e], send_sem=go_send.at[to], recv_sem=go_recv.at[e],
            device_id=(c, to), device_id_type=MESH,
        ).start()

    kv[rows_of((0, 0, 0), SEQ), :] = kv_own[...]
    kv_first()

    row = lax.broadcasted_iota(jnp.int32, (SEQ, SEQ), 0)
    col = lax.broadcasted_iota(jnp.int32, (SEQ, SEQ), 1)
    lower = (col <= row).astype(BF16)

    def three(a):
        high = a.astype(BF16)
        mid = (a - high.astype(F32)).astype(BF16)
        low = (a - high.astype(F32) - mid.astype(F32)).astype(BF16)
        return high, mid, low

    cum[...] = sum(dot(lower, term, ((1,), (1,))) for term in three(decay_t[...]))
    cum_t[...] = sum(dot(term, lower, ((1,), (1,))) for term in three(decay_t[...]))
    last = cum[SEQ - 1 : SEQ, :]
    line = lax.broadcasted_iota(jnp.int32, (16, HEAD), 0)
    for h in range(HEADS):
        tail = jnp.exp(last[:, h : h + 1] - cum[:, h : h + 1])
        head = pl.ds(h * HEAD, HEAD)
        scaled = lin_k[:, head].astype(F32) * tail
        state = dot_split(scaled.T, lin_v[:, head])
        high, mid, low = (jnp.broadcast_to(t.astype(F32), (16, HEAD)) for t in three(last[:, h : h + 1]))
        logs = jnp.where(line == 0, high, jnp.where(line == 1, mid, jnp.where(line == 2, low, 0.0))).astype(BF16)
        for i in range(4):
            state_out[4 * h + i, 0:32, :] = state[32 * i : 32 * i + 32].astype(BF16)
            state_out[4 * h + i, 32:48, :] = logs

    @pl.loop(1, CTX)
    def _(k):
        to = (c + k) % CTX
        pltpu.make_async_remote_copy(
            src_ref=state_out.at[to], dst_ref=state_in.at[c], send_sem=st_send.at[to], recv_sem=st_recv.at[c],
            device_id=(to, e), device_id_type=MESH,
        ).start()

    state_in[c] = state_out[c]

    kv_arrive((0, 0, 1), (0, 1, 0), (0, -1, 0), (1, 0, 0), (-1, 0, 0))

    got[e] = slabs[e]

    @pl.loop(1, EXPERTS)
    def _(k):
        at = (e + k) % EXPERTS
        pltpu.make_async_remote_copy(
            src_ref=slabs.at[at], dst_ref=got.at[at], send_sem=go_send.at[at], recv_sem=go_recv.at[at],
            device_id=(c, at), device_id_type=MESH,
        ).wait()

    for i in range(EXPERTS):
        wide[2 * i : 2 * i + 2, :] = got[i].astype(F32)
    tok[rows_of((0, 0, 0), ROWS), :] = wide[...].astype(BF16)
    tok_first()

    kv_arrive((0, 1, 1), (0, -1, 1), (1, 0, 1), (-1, 0, 1), (0, 2, 0), (0, 2, 1))
    kv_arrive(*((ds, df, 0) for df in (1, -1) for ds in (1, -1)))
    tok_arrive((0, 0, 1), (0, 1, 0), (0, -1, 0), (1, 0, 0), (-1, 0, 0))
    kv_arrive(*((ds, df, 1) for df in (1, -1) for ds in (1, -1)))
    kv_arrive(*((ds, 2, dz) for dz in (0, 1) for ds in (1, -1)))
    kv_arrive(*((2, df, dz) for df in (0, 1, -1, 2) for dz in (0, 1)))
    tok_arrive((0, 1, 1), (0, -1, 1))

    @pl.loop(1, CTX)
    def _(k):
        at = (c + k) % CTX
        pltpu.make_async_remote_copy(
            src_ref=state_out.at[at], dst_ref=state_in.at[at], send_sem=st_send.at[at], recv_sem=st_recv.at[at],
            device_id=(at, e), device_id_type=MESH,
        ).wait()

    def hop(i, run):
        prior_out[i] = run.astype(BF16)
        logs = jnp.sum(state_in[i, 32:48, :].astype(F32), axis=0, keepdims=True)
        return jnp.exp(logs) * run + state_in[i, 0:32, :].astype(F32)

    lax.fori_loop(0, CTX, hop, jnp.zeros((32, HEAD), F32))

    @pl.loop(1, CTX)
    def _(k):
        to = (c + k) % CTX
        pltpu.make_async_remote_copy(
            src_ref=prior_out.at[to], dst_ref=prior.at[c], send_sem=pr_send.at[to], recv_sem=pr_recv.at[c],
            device_id=(to, e), device_id_type=MESH,
        ).start()

    prior[c] = prior_out[c]

    wide_col = lax.broadcasted_iota(jnp.int32, (8, CTX * SEQ), 1)
    blk = jnp.right_shift(wide_col, 7)
    b_s, b_f, b_z = jnp.right_shift(blk, 3), jnp.bitwise_and(jnp.right_shift(blk, 1), 3), jnp.bitwise_and(blk, 1)
    b_ctx = (b_s + core * (b_f - b_s)) * 8 + b_z * 4 + b_f + core * (b_s - b_f)
    place = b_ctx * SEQ + jnp.bitwise_and(wide_col, SEQ - 1)
    line8 = lax.broadcasted_iota(jnp.int32, (8, CTX * SEQ), 0)

    @pl.loop(0, SEQ // 8)
    def _(i):
        bias[pl.ds(pl.multiple_of(i * 8, 8), 8), :] = jnp.where(place <= c * SEQ + i * 8 + line8, 0.0, -1e30)

    def attend(first, count):
        @pl.loop(first, first + count)
        def _(h):
            head = pl.ds(pl.multiple_of(h * HEAD, HEAD), HEAD)
            scores = dot(soft_q[:, head], kv[:, 0:HEAD], ((1,), (1,))) * SCALE + bias[...]
            top = jnp.max(scores, axis=1, keepdims=True)
            probs = jnp.exp(scores - top)
            total = jnp.sum(probs, axis=1, keepdims=True)
            mixed = dot(probs.astype(BF16), kv[:, HEAD : 2 * HEAD])
            soft_out[:, head] = (mixed / total).astype(BF16)

    def finish_lightning(heads):
        for h in heads:
            head = pl.ds(h * HEAD, HEAD)
            here = cum[:, h : h + 1]
            spread = here - cum_t[h : h + 1, :]
            decays = jnp.where(col <= row, jnp.exp(jnp.where(col <= row, spread, 0.0)), 0.0)
            scores = dot(lin_q[:, head], lin_k[:, head], ((1,), (1,))) * SCALE
            within = dot_split(scores * decays, lin_v[:, head])
            before = prior[4 * h : 4 * h + 4].reshape(HEAD, HEAD)
            combined = within + jnp.exp(here) * dot(lin_q[:, head], before) * SCALE
            root = jnp.sqrt(jnp.mean(combined * combined, axis=1, keepdims=True) + 1e-06)
            lin_out[:, head] = (combined / root * gain[:, head]).astype(BF16)

    chunk = 1024

    def group(ds):
        return pl.ds(pl.multiple_of((s + ds + 4) % 4 * 8 * ROWS, 8 * ROWS), 8 * ROWS)

    def enter(ds):
        def add(k, sums):
            at = pl.ds(pl.multiple_of(k * chunk, chunk), chunk)
            tokens = tok[group(ds), at]
            return (
                sums[0] + dot(tokens, gate[:, at], ((1,), (1,))),
                sums[1] + dot(tokens, up[:, at], ((1,), (1,))),
            )

        zero = jnp.zeros((8 * ROWS, FF), F32)
        a, b = lax.fori_loop(0, D // chunk, add, (zero, zero))
        hidden[group(ds), :] = (a / (1.0 + jnp.exp(-a)) * b).astype(BF16)

    def leave(ds):
        @pl.loop(0, D // chunk)
        def _(k):
            at = pl.ds(pl.multiple_of(k * chunk, chunk), chunk)
            part[group(ds), at] = dot(hidden[group(ds), :], down[:, at]).astype(BF16)

    attend(0, 1)
    tok_arrive((1, 0, 1), (-1, 0, 1), (0, 2, 0), (0, 2, 1))
    attend(1, 1)
    tok_arrive(*((ds, df, 0) for df in (1, -1) for ds in (1, -1)))
    attend(2, 1)
    attend(3, 1)
    tok_arrive(*((ds, df, 1) for df in (1, -1) for ds in (1, -1)))
    attend(4, 2)
    for copy in weights:
        copy.wait()
    enter(0)
    tok_arrive(*((ds, 2, dz) for dz in (0, 1) for ds in (1, -1)))
    attend(6, 2)
    enter(1)
    enter(-1)
    tok_arrive(*((2, df, dz) for df in (0, 1, -1, 2) for dz in (0, 1)))
    enter(2)

    rs_used = [0]

    def send_part(step, dst, sem, to):
        push(part.at[rows_of(step, ROWS)], dst, rs_send.at[rs_used[0]], sem, (ctx_of(to), e))
        rs_used[0] += 1

    def block(ref, i):
        return ref.at[pl.ds(i * ROWS, ROWS)]

    def add_in(step, *blocks):
        where = rows_of(step, ROWS)
        total = part[where, :].astype(F32)
        for b in blocks:
            total = total + b[...].astype(F32)
        part[where, :] = total.astype(BF16)

    leave(2)
    for i, df in enumerate(DFS):
        send_part((2, df, 0), block(s1r, 2 * i), s1_sem.at[2 * i], (-1, 0, 0))
        send_part((2, df, 1), block(s1r, 2 * i + 1), s1_sem.at[2 * i + 1], (1, 0, 0))
    leave(-1)
    for i, df in enumerate(DFS):
        send_part((-1, df, 1), block(s2r, 4 * i + 1), s2_sem.at[4 * i + 1], (-1, 0, 0))
    leave(1)
    for i, df in enumerate(DFS):
        send_part((1, df, 0), block(s2r, 4 * i + 2), s2_sem.at[4 * i + 2], (1, 0, 0))
    leave(0)

    @pl.loop(1, CTX)
    def _(k):
        at = (c + k) % CTX
        pltpu.make_async_remote_copy(
            src_ref=prior_out.at[at], dst_ref=prior.at[at], send_sem=pr_send.at[at], recv_sem=pr_recv.at[at],
            device_id=(at, e), device_id_type=MESH,
        ).wait()

    for i, df in enumerate(DFS):
        for k, step, to in ((0, (-1, df, 0), (-1, 0, 0)), (1, (1, df, 1), (1, 0, 0))):
            landed(block(s1r, 2 * i + k), s1_sem.at[2 * i + k], rs_send.at[0])
            add_in(step, block(s1r, 2 * i + k))
            slot = 4 * i + (0 if k == 0 else 3)
            send_part(step, block(s2r, slot), s2_sem.at[slot], to)
        finish_lightning((2 * i, 2 * i + 1))

    for i, df in enumerate(DFS):
        for slot in (1, 2, 0, 3):
            landed(block(s2r, 4 * i + slot), s2_sem.at[4 * i + slot], rs_send.at[0])
        add_in((0, df, 0), block(s2r, 4 * i), block(s2r, 4 * i + 2))
        add_in((0, df, 1), block(s2r, 4 * i + 1), block(s2r, 4 * i + 3))
        if df == 2:
            send_part((0, 2, 0), block(f1r, 0), f1_sem.at[0], (0, -1, 0))
            send_part((0, 2, 1), block(f1r, 1), f1_sem.at[1], (0, 1, 0))
        elif df == 1:
            send_part((0, 1, 0), block(f2r, 2), f2_sem.at[2], (0, 1, 0))
        elif df == -1:
            send_part((0, -1, 1), block(f2r, 1), f2_sem.at[1], (0, -1, 0))
            for k, step, to in ((0, (0, -1, 0), (0, -1, 0)), (1, (0, 1, 1), (0, 1, 0))):
                landed(block(f1r, k), f1_sem.at[k], rs_send.at[0])
                add_in(step, block(f1r, k))
                slot = 0 if k == 0 else 3
                send_part(step, block(f2r, slot), f2_sem.at[slot], to)

    landed(block(f2r, 1), f2_sem.at[1], rs_send.at[0])
    landed(block(f2r, 3), f2_sem.at[3], rs_send.at[0])
    add_in((0, 0, 1), block(f2r, 1), block(f2r, 3))
    send_part((0, 0, 1), zr, z_sem.at[0], (0, 0, 1))
    landed(block(f2r, 0), f2_sem.at[0], rs_send.at[0])
    landed(block(f2r, 2), f2_sem.at[2], rs_send.at[0])
    wide[...] = (
        part[rows_of((0, 0, 0), ROWS), :].astype(F32)
        + block(f2r, 0)[...].astype(F32)
        + block(f2r, 2)[...].astype(F32)
    )
    landed(zr, z_sem.at[0], rs_send.at[0])
    wide[...] = wide[...] + zr[...].astype(F32)

    for i in range(EXPERTS):
        back[i] = wide[2 * i : 2 * i + 2, :].astype(BF16)

    @pl.loop(1, EXPERTS)
    def _(k):
        to = (e + k) % EXPERTS
        pltpu.make_async_remote_copy(
            src_ref=back.at[to], dst_ref=ret.at[e], send_sem=back_send.at[to], recv_sem=back_recv.at[e],
            device_id=(c, to), device_id_type=MESH,
        ).start()

    ret[e] = back[e]

    @pl.loop(1, EXPERTS)
    def _(k):
        at = (e + k) % EXPERTS
        pltpu.make_async_remote_copy(
            src_ref=back.at[at], dst_ref=ret.at[at], send_sem=back_send.at[at], recv_sem=back_recv.at[at],
            device_id=(c, at), device_id_type=MESH,
        ).wait()

    for copy in unfinished:
        copy.wait_send()


def on_device(
    lin_query,
    lin_key,
    lin_value,
    log_decay,
    lin_gain,
    moe_input,
    routes,
    route_weight,
    gate_weight,
    up_weight,
    down_weight,
    soft_query,
    soft_kv,
):
    vmem, any_ = pl.BlockSpec(memory_space=pltpu.VMEM), pl.BlockSpec(memory_space=pl.ANY)
    smem = pl.BlockSpec(memory_space=pltpu.SMEM)
    dma = pltpu.SemaphoreType.DMA
    ret, lin, soft = pl.pallas_call(
        kernel,
        out_shape=(
            jax.ShapeDtypeStruct((EXPERTS, CAP, D), BF16),
            jax.ShapeDtypeStruct((SEQ, HEADS * HEAD), BF16),
            jax.ShapeDtypeStruct((SEQ, HEADS * HEAD), BF16),
        ),
        in_specs=[smem, vmem, vmem, any_, any_, any_] + [vmem] * 6,
        out_specs=(vmem, vmem, vmem),
        scratch_shapes=[
            pltpu.VMEM((CTX * SEQ, 2 * HEAD), BF16),
            pltpu.VMEM((CTX * ROWS, D), BF16),
            pltpu.VMEM((CTX * ROWS, D), BF16),
            pltpu.VMEM((8 * ROWS, D), BF16),
            pltpu.VMEM((16 * ROWS, D), BF16),
            pltpu.VMEM((2 * ROWS, D), BF16),
            pltpu.VMEM((4 * ROWS, D), BF16),
            pltpu.VMEM((ROWS, D), BF16),
            pltpu.VMEM((EXPERTS, CAP, D), BF16),
            pltpu.VMEM((EXPERTS, CAP, D), BF16),
            pltpu.VMEM((EXPERTS, CAP, D), BF16),
            pltpu.VMEM((ROWS, D), F32),
            pltpu.VMEM((FF, D), BF16),
            pltpu.VMEM((FF, D), BF16),
            pltpu.VMEM((FF, D), BF16),
            pltpu.VMEM((CTX * ROWS, FF), BF16),
            pltpu.VMEM((SEQ, CTX * SEQ), F32),
            pltpu.VMEM((SEQ, HEADS), F32),
            pltpu.VMEM((HEADS, SEQ), F32),
            pltpu.VMEM((CTX, 48, HEAD), BF16),
            pltpu.VMEM((CTX, 48, HEAD), BF16),
            pltpu.VMEM((CTX, 32, HEAD), BF16),
            pltpu.VMEM((CTX, 32, HEAD), BF16),
            dma((3,)),
            dma((31,)), dma((32,)), dma((31,)), dma((32,)), dma((31,)),
            dma((8,)), dma((16,)), dma((2,)), dma((4,)), dma((1,)),
            dma((EXPERTS,)), dma((EXPERTS,)), dma((EXPERTS,)), dma((EXPERTS,)),
            dma((CTX,)), dma((CTX,)), dma((CTX,)), dma((CTX,)),
        ],
        compiler_params=pltpu.CompilerParams(
            collective_id=0, has_side_effects=True, vmem_limit_bytes=58 * 2**20
        ),
    )(
        routes.T,
        moe_input,
        soft_kv.reshape(SEQ, 2 * HEAD),
        gate_weight.reshape(D, FF).T,
        up_weight.reshape(D, FF).T,
        down_weight.reshape(FF, D),
        lin_query,
        lin_key,
        lin_value,
        log_decay.T,
        lin_gain.reshape(1, HEADS * HEAD),
        soft_query,
    )
    lin_out, moe_out, soft_out = pl.pallas_call(
        finish,
        out_shape=(
            jax.ShapeDtypeStruct((SEQ, HEADS * HEAD), BF16),
            jax.ShapeDtypeStruct(moe_input.shape, BF16),
            jax.ShapeDtypeStruct((SEQ, HEADS * HEAD), BF16),
        ),
        in_specs=[smem, smem, vmem, vmem, vmem],
        out_specs=(vmem, vmem, vmem),
        scratch_shapes=[pltpu.VMEM((ROWS, D), F32)],
    )(routes.T, route_weight.T, ret, lin, soft)
    return (lin_out, moe_out, soft_out)


def solution(mesh):
    placed = (
        P("ctx", "exp"),
        P("ctx", "exp"),
        P("ctx", "exp"),
        P("ctx", "exp"),
        P("exp"),
        P(("ctx", "exp"), None),
        P(("ctx", "exp"), None),
        P(("ctx", "exp"), None),
        P("exp", None, "ctx"),
        P("exp", None, "ctx"),
        P("exp", "ctx", None),
        P("ctx", "exp"),
        P("ctx", "exp", None, None),
    )
    return jax.shard_map(
        on_device,
        mesh=mesh,
        in_specs=placed,
        out_specs=(P("ctx", "exp"), P(("ctx", "exp"), None), P("ctx", "exp")),
        check_vma=False,
    )
```

```python
import math

import jax
import jax.numpy as jnp
from jax import lax
from jax.experimental import pallas as pl
from jax.experimental.pallas import tpu as pltpu
from jax.sharding import PartitionSpec as P

D = 6144
HEAD = 128
EXPERTS = 8
TOP = 2
CAP = 2
CTX = 32
SEQ = 128
HEADS = 8
FF = 288
ROWS = 16
SCALE = 1.0 / math.sqrt(HEAD)
F32, BF16 = jnp.float32, jnp.bfloat16
MESH = pl.DeviceIdType.MESH
DFS = (2, 1, -1, 0)


def dot(a, b, dims=((1,), (0,))):
    return lax.dot_general(a, b, (dims, ((), ())), preferred_element_type=F32)


def dot_split(a, b, dims=((1,), (0,))):
    high = a.astype(BF16)
    low = (a - high.astype(F32)).astype(BF16)
    return dot(high, b, dims) + dot(low, b, dims)


def slots_of(routes):
    line = lax.broadcasted_iota(jnp.int32, (ROWS, 1), 0)
    expert, place = jnp.right_shift(line, 1), jnp.bitwise_and(line, 1)
    met = jnp.zeros((ROWS, 1), jnp.int32)
    found = []
    for r in range(6):
        named = (expert == routes[0, r]) | (expert == routes[1, r])
        found.append((expert, named & (met == place)))
        met = met + named.astype(jnp.int32)
    return found


def finish(routes, weights, ret, lin, soft, lin_out, moe_out, soft_out, wide):
    lin_out[...] = lin[...]
    soft_out[...] = soft[...]
    for i in range(EXPERTS):
        wide[2 * i : 2 * i + 2, :] = ret[i].astype(F32)
    for r, (expert, taken) in enumerate(slots_of(routes)):
        weight = jnp.where(expert == routes[0, r], weights[0, r], weights[1, r])
        mixed = jnp.sum(jnp.where(taken, weight, 0.0) * wide[...], axis=0, keepdims=True)
        moe_out[r : r + 1, :] = mixed.astype(BF16)


def kernel(
    routes, moe_in, kv_own, gate_hbm, up_hbm, down_hbm, lin_q, lin_k, lin_v, decay_t, gain, soft_q,
    ret, lin_out, soft_out,
    kv, tok, part, s1r, s2r, f1r, f2r, zr, slabs, got, back, wide, gate, up, down, hidden,
    bias, cum, cum_t, state_out, state_in, prior_out, prior,
    w_sem, kv_send, kv_recv, tok_send, tok_recv, rs_send, s1_sem, s2_sem, f1_sem, f2_sem, z_sem,
    go_send, go_recv, back_send, back_recv, st_send, st_recv, pr_send, pr_recv,
):
    c, e = lax.axis_index("ctx"), lax.axis_index("exp")
    y, z, x, core = c // 8, (c // 4) % 2, c % 4, e % 2
    f, s = x + core * (y - x), y + core * (x - y)

    def rel(step):
        ds, df, dz = step
        return (s + ds + 4) % 4, (f + df + 4) % 4, (z + dz) % 2

    def ctx_of(step):
        ss, ff, zz = rel(step)
        return (ss + core * (ff - ss)) * 8 + zz * 4 + ff + core * (ss - ff)

    def index_of(step):
        ss, ff, zz = rel(step)
        return ss * 8 + ff * 2 + zz

    def rows_of(step, rows):
        return pl.ds(pl.multiple_of(index_of(step) * rows, rows), rows)

    barrier = pltpu.get_barrier_semaphore()

    @pl.loop(1, CTX)
    def _(k):
        pl.semaphore_signal(barrier, inc=1, device_id=((c + k) % CTX, e), device_id_type=MESH)

    @pl.loop(1, EXPERTS)
    def _(k):
        pl.semaphore_signal(barrier, inc=1, device_id=(c, (e + k) % EXPERTS), device_id_type=MESH)

    pl.semaphore_wait(barrier, CTX - 1 + EXPERTS - 1)

    weights = [
        pltpu.make_async_copy(src, dst, w_sem.at[i])
        for i, (src, dst) in enumerate(((gate_hbm, gate), (up_hbm, up), (down_hbm, down)))
    ]
    for copy in weights:
        copy.start()

    unfinished = []

    def push(src, dst, send_sem, recv_sem, to):
        copy = pltpu.make_async_remote_copy(
            src_ref=src, dst_ref=dst, send_sem=send_sem, recv_sem=recv_sem, device_id=to, device_id_type=MESH
        )
        copy.start()
        unfinished.append(copy)

    def landed(ref, recv_sem, spare_sem):
        pltpu.make_async_remote_copy(
            src_ref=ref, dst_ref=ref, send_sem=spare_sem, recv_sem=recv_sem,
            device_id=(ctx_of((0, 0, 1)), e), device_id_type=MESH,
        ).wait_recv()

    def gather(buf, rows, send_sems, recv_sems):
        used = [0]

        def send(step, to):
            where = rows_of(step, rows)
            push(buf.at[where], buf.at[where], send_sems.at[used[0]], recv_sems.at[index_of(step)], (ctx_of(to), e))
            used[0] += 1

        def sideways(step):
            send(step, (1, 0, 0))
            send(step, (-1, 0, 0))

        def own():
            send((0, 0, 0), (0, 0, 1))
            send((0, 0, 0), (0, 1, 0))
            send((0, 0, 0), (0, -1, 0))
            sideways((0, 0, 0))

        def arrive(*steps):
            for step in steps:
                ds, df, dz = step
                landed(buf.at[rows_of(step, rows)], recv_sems.at[index_of(step)], send_sems.at[0])
                if ds == 0:
                    if df == 0:
                        send(step, (0, 1, 0))
                        send(step, (0, -1, 0))
                    elif df == -1 and dz == 0:
                        send(step, (0, 1, 0))
                    elif df == 1 and dz == 1:
                        send(step, (0, -1, 0))
                    sideways(step)
                elif ds == -1 and dz == 0:
                    send(step, (1, 0, 0))
                elif ds == 1 and dz == 1:
                    send(step, (-1, 0, 0))

        return own, arrive

    kv_used = [0]

    def kv_put(step, to, half=None):
        where = rows_of(step, SEQ)
        if half is not None:
            where = pl.ds(pl.multiple_of(index_of(step) * SEQ + half * (SEQ // 2), SEQ // 2), SEQ // 2)
        sem = kv_recv.at[2 * index_of(step) + (half or 0)]
        push(kv.at[where], kv.at[where], kv_send.at[kv_used[0]], sem, (ctx_of(to), e))
        kv_used[0] += 1

    def kv_arrive(*steps):
        for ds, df, dz in steps:
            at = index_of((ds, df, dz))
            if dz == 0 and (ds == 2 or (ds == 0 and df == 2)):
                for half in (0, 1):
                    where = pl.ds(pl.multiple_of(at * SEQ + half * (SEQ // 2), SEQ // 2), SEQ // 2)
                    landed(kv.at[where], kv_recv.at[2 * at + half], kv_send.at[0])
            elif (ds, df, dz) != (0, 0, 0):
                landed(kv.at[rows_of((ds, df, dz), SEQ)], kv_recv.at[2 * at], kv_send.at[0])
            if dz == 1:
                continue
            step = (ds, df, 0)
            if ds == 0:
                if df == 0:
                    kv_put(step, (0, 1, 0))
                    kv_put(step, (0, -1, 0))
                elif df == -1:
                    kv_put(step, (0, 1, 0), 0)
                elif df == 1:
                    kv_put(step, (0, -1, 0), 1)
                kv_put(step, (1, 0, 0))
                kv_put(step, (-1, 0, 0))
            elif ds == -1:
                kv_put(step, (1, 0, 0), 0)
            elif ds == 1:
                kv_put(step, (-1, 0, 0), 1)
            kv_put(step, (0, 0, 1))

    tok_first, tok_arrive = gather(tok, ROWS, tok_send, tok_recv)

    wide[...] = sum(
        taken.astype(F32) * moe_in[r : r + 1, :].astype(F32) for r, (_, taken) in enumerate(slots_of(routes))
    )
    for i in range(EXPERTS):
        slabs[i] = wide[2 * i : 2 * i + 2, :].astype(BF16)

    @pl.loop(1, EXPERTS)
    def _(k):
        to = (e + k) % EXPERTS
        pltpu.make_async_remote_copy(
            src_ref=slabs.at[to], dst_ref=got.at[e], send_sem=go_send.at[to], recv_sem=go_recv.at[e],
            device_id=(c, to), device_id_type=MESH,
        ).start()

    kv[rows_of((0, 0, 0), SEQ), :] = kv_own[...]
    kv_arrive((0, 0, 0))

    row = lax.broadcasted_iota(jnp.int32, (SEQ, SEQ), 0)
    col = lax.broadcasted_iota(jnp.int32, (SEQ, SEQ), 1)
    lower = (col <= row).astype(BF16)

    def three(a):
        high = a.astype(BF16)
        mid = (a - high.astype(F32)).astype(BF16)
        low = (a - high.astype(F32) - mid.astype(F32)).astype(BF16)
        return high, mid, low

    cum[...] = sum(dot(lower, term, ((1,), (1,))) for term in three(decay_t[...]))
    cum_t[...] = sum(dot(term, lower, ((1,), (1,))) for term in three(decay_t[...]))
    last = cum[SEQ - 1 : SEQ, :]
    line = lax.broadcasted_iota(jnp.int32, (16, HEAD), 0)
    for h in range(HEADS):
        tail = jnp.exp(last[:, h : h + 1] - cum[:, h : h + 1])
        head = pl.ds(h * HEAD, HEAD)
        scaled = lin_k[:, head].astype(F32) * tail
        state = dot_split(scaled.T, lin_v[:, head])
        high, mid, low = (jnp.broadcast_to(t.astype(F32), (16, HEAD)) for t in three(last[:, h : h + 1]))
        logs = jnp.where(line == 0, high, jnp.where(line == 1, mid, jnp.where(line == 2, low, 0.0))).astype(BF16)
        for i in range(4):
            state_out[4 * h + i, 0:32, :] = state[32 * i : 32 * i + 32].astype(BF16)
            state_out[4 * h + i, 32:48, :] = logs

    @pl.loop(1, CTX)
    def _(k):
        to = (c + k) % CTX
        pltpu.make_async_remote_copy(
            src_ref=state_out.at[to], dst_ref=state_in.at[c], send_sem=st_send.at[to], recv_sem=st_recv.at[c],
            device_id=(to, e), device_id_type=MESH,
        ).start()

    state_in[c] = state_out[c]

    kv_arrive((0, 1, 0), (0, -1, 0))

    got[e] = slabs[e]

    @pl.loop(1, EXPERTS)
    def _(k):
        at = (e + k) % EXPERTS
        pltpu.make_async_remote_copy(
            src_ref=slabs.at[at], dst_ref=got.at[at], send_sem=go_send.at[at], recv_sem=go_recv.at[at],
            device_id=(c, at), device_id_type=MESH,
        ).wait()

    for i in range(EXPERTS):
        wide[2 * i : 2 * i + 2, :] = got[i].astype(F32)
    tok[rows_of((0, 0, 0), ROWS), :] = wide[...].astype(BF16)
    tok_first()

    wide_col = lax.broadcasted_iota(jnp.int32, (8, CTX * SEQ), 1)
    blk = jnp.right_shift(wide_col, 7)
    b_s, b_f, b_z = jnp.right_shift(blk, 3), jnp.bitwise_and(jnp.right_shift(blk, 1), 3), jnp.bitwise_and(blk, 1)
    b_ctx = (b_s + core * (b_f - b_s)) * 8 + b_z * 4 + b_f + core * (b_s - b_f)
    place = b_ctx * SEQ + jnp.bitwise_and(wide_col, SEQ - 1)
    line8 = lax.broadcasted_iota(jnp.int32, (8, CTX * SEQ), 0)

    @pl.loop(0, SEQ // 8)
    def _(i):
        bias[pl.ds(pl.multiple_of(i * 8, 8), 8), :] = jnp.where(place <= c * SEQ + i * 8 + line8, 0.0, -1e30)

    def attend(first, count):
        @pl.loop(first, first + count)
        def _(h):
            head = pl.ds(pl.multiple_of(h * HEAD, HEAD), HEAD)
            scores = dot(soft_q[:, head], kv[:, 0:HEAD], ((1,), (1,))) * SCALE + bias[...]
            top = jnp.max(scores, axis=1, keepdims=True)
            probs = jnp.exp(scores - top)
            total = jnp.sum(probs, axis=1, keepdims=True)
            mixed = dot(probs.astype(BF16), kv[:, HEAD : 2 * HEAD])
            soft_out[:, head] = (mixed / total).astype(BF16)

    def finish_lightning(heads):
        for h in heads:
            head = pl.ds(h * HEAD, HEAD)
            here = cum[:, h : h + 1]
            spread = here - cum_t[h : h + 1, :]
            decays = jnp.where(col <= row, jnp.exp(jnp.where(col <= row, spread, 0.0)), 0.0)
            scores = dot(lin_q[:, head], lin_k[:, head], ((1,), (1,))) * SCALE
            within = dot_split(scores * decays, lin_v[:, head])
            before = prior[4 * h : 4 * h + 4].reshape(HEAD, HEAD)
            combined = within + jnp.exp(here) * dot(lin_q[:, head], before) * SCALE
            root = jnp.sqrt(jnp.mean(combined * combined, axis=1, keepdims=True) + 1e-06)
            lin_out[:, head] = (combined / root * gain[:, head]).astype(BF16)

    chunk = 1024

    def group(ds):
        return pl.ds(pl.multiple_of((s + ds + 4) % 4 * 8 * ROWS, 8 * ROWS), 8 * ROWS)

    def enter(ds):
        def add(k, sums):
            at = pl.ds(pl.multiple_of(k * chunk, chunk), chunk)
            tokens = tok[group(ds), at]
            return (
                sums[0] + dot(tokens, gate[:, at], ((1,), (1,))),
                sums[1] + dot(tokens, up[:, at], ((1,), (1,))),
            )

        zero = jnp.zeros((8 * ROWS, FF), F32)
        a, b = lax.fori_loop(0, D // chunk, add, (zero, zero))
        hidden[group(ds), :] = (a / (1.0 + jnp.exp(-a)) * b).astype(BF16)

    def leave(ds):
        @pl.loop(0, D // chunk)
        def _(k):
            at = pl.ds(pl.multiple_of(k * chunk, chunk), chunk)
            part[group(ds), at] = dot(hidden[group(ds), :], down[:, at]).astype(BF16)

    def pairs(df, dz):
        return (1, df, dz), (-1, df, dz)

    kv_arrive(*pairs(0, 0), (0, 2, 0))
    tok_arrive((0, 0, 1), (0, 1, 0), (0, -1, 0))
    kv_arrive(*pairs(1, 0), *pairs(-1, 0))
    tok_arrive(*pairs(0, 0))
    kv_arrive(*pairs(2, 0))
    tok_arrive((0, 1, 1), (0, -1, 1))
    kv_arrive((2, 0, 0), (2, 1, 0))
    tok_arrive(*pairs(0, 1), (0, 2, 0), (0, 2, 1))
    kv_arrive((2, -1, 0), (2, 2, 0))
    tok_arrive(*pairs(1, 0), *pairs(-1, 0))
    tok_arrive(*pairs(1, 1), *pairs(-1, 1))
    for copy in weights:
        copy.wait()
    enter(0)
    tok_arrive(*pairs(2, 0), *pairs(2, 1))
    enter(1)
    enter(-1)
    kv_arrive(*((ds, df, 1) for ds in (0, 1, -1, 2) for df in (0, 1, -1, 2)))

    @pl.loop(1, CTX)
    def _(k):
        at = (c + k) % CTX
        pltpu.make_async_remote_copy(
            src_ref=state_out.at[at], dst_ref=state_in.at[at], send_sem=st_send.at[at], recv_sem=st_recv.at[at],
            device_id=(at, e), device_id_type=MESH,
        ).wait()

    def hop(i, run):
        prior_out[i] = run.astype(BF16)
        logs = jnp.sum(state_in[i, 32:48, :].astype(F32), axis=0, keepdims=True)
        return jnp.exp(logs) * run + state_in[i, 0:32, :].astype(F32)

    lax.fori_loop(0, CTX, hop, jnp.zeros((32, HEAD), F32))

    @pl.loop(1, CTX)
    def _(k):
        to = (c + k) % CTX
        pltpu.make_async_remote_copy(
            src_ref=prior_out.at[to], dst_ref=prior.at[c], send_sem=pr_send.at[to], recv_sem=pr_recv.at[c],
            device_id=(to, e), device_id_type=MESH,
        ).start()

    prior[c] = prior_out[c]

    tok_arrive(*((2, df, dz) for df in (0, 1, -1, 2) for dz in (0, 1)))
    enter(2)

    rs_used = [0]

    def send_part(step, dst, sem, to):
        push(part.at[rows_of(step, ROWS)], dst, rs_send.at[rs_used[0]], sem, (ctx_of(to), e))
        rs_used[0] += 1

    def block(ref, i):
        return ref.at[pl.ds(i * ROWS, ROWS)]

    def add_in(step, *blocks):
        where = rows_of(step, ROWS)
        total = part[where, :].astype(F32)
        for b in blocks:
            total = total + b[...].astype(F32)
        part[where, :] = total.astype(BF16)

    leave(2)
    for i, df in enumerate(DFS):
        send_part((2, df, 0), block(s1r, 2 * i), s1_sem.at[2 * i], (-1, 0, 0))
        send_part((2, df, 1), block(s1r, 2 * i + 1), s1_sem.at[2 * i + 1], (1, 0, 0))
    leave(-1)
    for i, df in enumerate(DFS):
        send_part((-1, df, 1), block(s2r, 4 * i + 1), s2_sem.at[4 * i + 1], (-1, 0, 0))
    leave(1)
    for i, df in enumerate(DFS):
        send_part((1, df, 0), block(s2r, 4 * i + 2), s2_sem.at[4 * i + 2], (1, 0, 0))
    leave(0)

    for i, df in enumerate(DFS):
        for k, step, to in ((0, (-1, df, 0), (-1, 0, 0)), (1, (1, df, 1), (1, 0, 0))):
            landed(block(s1r, 2 * i + k), s1_sem.at[2 * i + k], rs_send.at[0])
            add_in(step, block(s1r, 2 * i + k))
            slot = 4 * i + (0 if k == 0 else 3)
            send_part(step, block(s2r, slot), s2_sem.at[slot], to)
        attend(2 * i, 2)

    @pl.loop(1, CTX)
    def _(k):
        at = (c + k) % CTX
        pltpu.make_async_remote_copy(
            src_ref=prior_out.at[at], dst_ref=prior.at[at], send_sem=pr_send.at[at], recv_sem=pr_recv.at[at],
            device_id=(at, e), device_id_type=MESH,
        ).wait()

    finish_lightning(range(HEADS))

    for i, df in enumerate(DFS):
        for slot in (1, 2, 0, 3):
            landed(block(s2r, 4 * i + slot), s2_sem.at[4 * i + slot], rs_send.at[0])
        add_in((0, df, 0), block(s2r, 4 * i), block(s2r, 4 * i + 2))
        add_in((0, df, 1), block(s2r, 4 * i + 1), block(s2r, 4 * i + 3))
        if df == 2:
            send_part((0, 2, 0), block(f1r, 0), f1_sem.at[0], (0, -1, 0))
            send_part((0, 2, 1), block(f1r, 1), f1_sem.at[1], (0, 1, 0))
        elif df == 1:
            send_part((0, 1, 0), block(f2r, 2), f2_sem.at[2], (0, 1, 0))
        elif df == -1:
            send_part((0, -1, 1), block(f2r, 1), f2_sem.at[1], (0, -1, 0))
            for k, step, to in ((0, (0, -1, 0), (0, -1, 0)), (1, (0, 1, 1), (0, 1, 0))):
                landed(block(f1r, k), f1_sem.at[k], rs_send.at[0])
                add_in(step, block(f1r, k))
                slot = 0 if k == 0 else 3
                send_part(step, block(f2r, slot), f2_sem.at[slot], to)

    landed(block(f2r, 1), f2_sem.at[1], rs_send.at[0])
    landed(block(f2r, 3), f2_sem.at[3], rs_send.at[0])
    add_in((0, 0, 1), block(f2r, 1), block(f2r, 3))
    send_part((0, 0, 1), zr, z_sem.at[0], (0, 0, 1))
    landed(block(f2r, 0), f2_sem.at[0], rs_send.at[0])
    landed(block(f2r, 2), f2_sem.at[2], rs_send.at[0])
    wide[...] = (
        part[rows_of((0, 0, 0), ROWS), :].astype(F32)
        + block(f2r, 0)[...].astype(F32)
        + block(f2r, 2)[...].astype(F32)
    )
    landed(zr, z_sem.at[0], rs_send.at[0])
    wide[...] = wide[...] + zr[...].astype(F32)

    for i in range(EXPERTS):
        back[i] = wide[2 * i : 2 * i + 2, :].astype(BF16)

    @pl.loop(1, EXPERTS)
    def _(k):
        to = (e + k) % EXPERTS
        pltpu.make_async_remote_copy(
            src_ref=back.at[to], dst_ref=ret.at[e], send_sem=back_send.at[to], recv_sem=back_recv.at[e],
            device_id=(c, to), device_id_type=MESH,
        ).start()

    ret[e] = back[e]

    @pl.loop(1, EXPERTS)
    def _(k):
        at = (e + k) % EXPERTS
        pltpu.make_async_remote_copy(
            src_ref=back.at[at], dst_ref=ret.at[at], send_sem=back_send.at[at], recv_sem=back_recv.at[at],
            device_id=(c, at), device_id_type=MESH,
        ).wait()

    for copy in unfinished:
        copy.wait_send()


def on_device(
    lin_query,
    lin_key,
    lin_value,
    log_decay,
    lin_gain,
    moe_input,
    routes,
    route_weight,
    gate_weight,
    up_weight,
    down_weight,
    soft_query,
    soft_kv,
):
    vmem, any_ = pl.BlockSpec(memory_space=pltpu.VMEM), pl.BlockSpec(memory_space=pl.ANY)
    smem = pl.BlockSpec(memory_space=pltpu.SMEM)
    dma = pltpu.SemaphoreType.DMA
    ret, lin, soft = pl.pallas_call(
        kernel,
        out_shape=(
            jax.ShapeDtypeStruct((EXPERTS, CAP, D), BF16),
            jax.ShapeDtypeStruct((SEQ, HEADS * HEAD), BF16),
            jax.ShapeDtypeStruct((SEQ, HEADS * HEAD), BF16),
        ),
        in_specs=[smem, vmem, vmem, any_, any_, any_] + [vmem] * 6,
        out_specs=(vmem, vmem, vmem),
        scratch_shapes=[
            pltpu.VMEM((CTX * SEQ, 2 * HEAD), BF16),
            pltpu.VMEM((CTX * ROWS, D), BF16),
            pltpu.VMEM((CTX * ROWS, D), BF16),
            pltpu.VMEM((8 * ROWS, D), BF16),
            pltpu.VMEM((16 * ROWS, D), BF16),
            pltpu.VMEM((2 * ROWS, D), BF16),
            pltpu.VMEM((4 * ROWS, D), BF16),
            pltpu.VMEM((ROWS, D), BF16),
            pltpu.VMEM((EXPERTS, CAP, D), BF16),
            pltpu.VMEM((EXPERTS, CAP, D), BF16),
            pltpu.VMEM((EXPERTS, CAP, D), BF16),
            pltpu.VMEM((ROWS, D), F32),
            pltpu.VMEM((FF, D), BF16),
            pltpu.VMEM((FF, D), BF16),
            pltpu.VMEM((FF, D), BF16),
            pltpu.VMEM((CTX * ROWS, FF), BF16),
            pltpu.VMEM((SEQ, CTX * SEQ), F32),
            pltpu.VMEM((SEQ, HEADS), F32),
            pltpu.VMEM((HEADS, SEQ), F32),
            pltpu.VMEM((CTX, 48, HEAD), BF16),
            pltpu.VMEM((CTX, 48, HEAD), BF16),
            pltpu.VMEM((CTX, 32, HEAD), BF16),
            pltpu.VMEM((CTX, 32, HEAD), BF16),
            dma((3,)),
            dma((36,)), dma((64,)), dma((31,)), dma((32,)), dma((31,)),
            dma((8,)), dma((16,)), dma((2,)), dma((4,)), dma((1,)),
            dma((EXPERTS,)), dma((EXPERTS,)), dma((EXPERTS,)), dma((EXPERTS,)),
            dma((CTX,)), dma((CTX,)), dma((CTX,)), dma((CTX,)),
        ],
        compiler_params=pltpu.CompilerParams(
            collective_id=0, has_side_effects=True, vmem_limit_bytes=58 * 2**20
        ),
    )(
        routes.T,
        moe_input,
        soft_kv.reshape(SEQ, 2 * HEAD),
        gate_weight.reshape(D, FF).T,
        up_weight.reshape(D, FF).T,
        down_weight.reshape(FF, D),
        lin_query,
        lin_key,
        lin_value,
        log_decay.T,
        lin_gain.reshape(1, HEADS * HEAD),
        soft_query,
    )
    lin_out, moe_out, soft_out = pl.pallas_call(
        finish,
        out_shape=(
            jax.ShapeDtypeStruct((SEQ, HEADS * HEAD), BF16),
            jax.ShapeDtypeStruct(moe_input.shape, BF16),
            jax.ShapeDtypeStruct((SEQ, HEADS * HEAD), BF16),
        ),
        in_specs=[smem, smem, vmem, vmem, vmem],
        out_specs=(vmem, vmem, vmem),
        scratch_shapes=[pltpu.VMEM((ROWS, D), F32)],
    )(routes.T, route_weight.T, ret, lin, soft)
    return (lin_out, moe_out, soft_out)


def solution(mesh):
    placed = (
        P("ctx", "exp"),
        P("ctx", "exp"),
        P("ctx", "exp"),
        P("ctx", "exp"),
        P("exp"),
        P(("ctx", "exp"), None),
        P(("ctx", "exp"), None),
        P(("ctx", "exp"), None),
        P("exp", None, "ctx"),
        P("exp", None, "ctx"),
        P("exp", "ctx", None),
        P("ctx", "exp"),
        P("ctx", "exp", None, None),
    )
    return jax.shard_map(
        on_device,
        mesh=mesh,
        in_specs=placed,
        out_specs=(P("ctx", "exp"), P(("ctx", "exp"), None), P("ctx", "exp")),
        check_vma=False,
    )
```

```python
import math

import jax
import jax.numpy as jnp
from jax import lax
from jax.experimental import pallas as pl
from jax.experimental.pallas import tpu as pltpu
from jax.sharding import PartitionSpec as P

D = 6144
HEAD = 128
EXPERTS = 8
TOP = 2
CAP = 2
CTX = 32
SEQ = 128
HEADS = 8
FF = 288
ROWS = 16
SCALE = 1.0 / math.sqrt(HEAD)
F32, BF16 = jnp.float32, jnp.bfloat16
MESH = pl.DeviceIdType.MESH
DFS = (2, 1, -1, 0)
MAIN, SIDE = 4096, 1024


def dot(a, b, dims=((1,), (0,))):
    return lax.dot_general(a, b, (dims, ((), ())), preferred_element_type=F32)


def dot_split(a, b, dims=((1,), (0,))):
    high = a.astype(BF16)
    low = (a - high.astype(F32)).astype(BF16)
    return dot(high, b, dims) + dot(low, b, dims)


def slots_of(routes):
    line = lax.broadcasted_iota(jnp.int32, (ROWS, 1), 0)
    expert, place = jnp.right_shift(line, 1), jnp.bitwise_and(line, 1)
    met = jnp.zeros((ROWS, 1), jnp.int32)
    found = []
    for r in range(6):
        named = (expert == routes[0, r]) | (expert == routes[1, r])
        found.append((expert, named & (met == place)))
        met = met + named.astype(jnp.int32)
    return found


def finish(routes, weights, ret, lin, soft, lin_out, moe_out, soft_out, wide):
    lin_out[...] = lin[...]
    soft_out[...] = soft[...]
    for i in range(EXPERTS):
        wide[2 * i : 2 * i + 2, :] = ret[i].astype(F32)
    for r, (expert, taken) in enumerate(slots_of(routes)):
        weight = jnp.where(expert == routes[0, r], weights[0, r], weights[1, r])
        mixed = jnp.sum(jnp.where(taken, weight, 0.0) * wide[...], axis=0, keepdims=True)
        moe_out[r : r + 1, :] = mixed.astype(BF16)


def kernel(
    routes, moe_in, kv_own, gate_hbm, up_hbm, down_hbm, lin_q, lin_k, lin_v, decay_t, gain, soft_q,
    ret, lin_out, soft_out,
    kv, tok, part, s1r, s2r, f1r, f2r, zr, zt, slabs, got, back, wide, gate, up, down, hidden,
    bias, cum, cum_t, state_out, state_in, prior_out, prior,
    w_sem, kv_send, kv_recv, tok_send, tok_recv, rs_send, s1_sem, s2_sem, f1_sem, f2_sem, z_sem,
    go_send, go_recv, back_send, back_recv, st_send, st_recv, pr_send, pr_recv,
):
    c, e = lax.axis_index("ctx"), lax.axis_index("exp")
    y, z, x, core = c // 8, (c // 4) % 2, c % 4, e % 2
    f, s = x + core * (y - x), y + core * (x - y)

    def rel(step):
        ds, df, dz = step
        return (s + ds + 4) % 4, (f + df + 4) % 4, (z + dz) % 2

    def ctx_of(step):
        ss, ff, zz = rel(step)
        return (ss + core * (ff - ss)) * 8 + zz * 4 + ff + core * (ss - ff)

    def index_of(step):
        ss, ff, zz = rel(step)
        return ss * 8 + ff * 2 + zz

    def rows_of(step, rows):
        return pl.ds(pl.multiple_of(index_of(step) * rows, rows), rows)

    barrier = pltpu.get_barrier_semaphore()

    @pl.loop(1, CTX)
    def _(k):
        pl.semaphore_signal(barrier, inc=1, device_id=((c + k) % CTX, e), device_id_type=MESH)

    @pl.loop(1, EXPERTS)
    def _(k):
        pl.semaphore_signal(barrier, inc=1, device_id=(c, (e + k) % EXPERTS), device_id_type=MESH)

    pl.semaphore_wait(barrier, CTX - 1 + EXPERTS - 1)

    weights = [
        pltpu.make_async_copy(src, dst, w_sem.at[i])
        for i, (src, dst) in enumerate(((gate_hbm, gate), (up_hbm, up), (down_hbm, down)))
    ]
    for copy in weights:
        copy.start()

    def push(src, dst, send_sem, recv_sem, to):
        pltpu.make_async_remote_copy(
            src_ref=src, dst_ref=dst, send_sem=send_sem, recv_sem=recv_sem, device_id=to, device_id_type=MESH
        ).start()

    def landed(ref, recv_sem, spare_sem):
        pltpu.make_async_remote_copy(
            src_ref=ref, dst_ref=ref, send_sem=spare_sem, recv_sem=recv_sem,
            device_id=(ctx_of((0, 0, 1)), e), device_id_type=MESH,
        ).wait_recv()

    def all_of(ref, send_sem, recv_sem):
        return pltpu.make_async_remote_copy(
            src_ref=ref, dst_ref=ref, send_sem=send_sem, recv_sem=recv_sem,
            device_id=(ctx_of((0, 0, 1)), e), device_id_type=MESH,
        )

    def gather(buf, rows, send_sems, recv_sems):
        def send(step, to):
            where = rows_of(step, rows)
            push(buf.at[where], buf.at[where], send_sems.at[0], recv_sems.at[index_of(step)], (ctx_of(to), e))

        def sideways(step):
            send(step, (1, 0, 0))
            send(step, (-1, 0, 0))

        def own():
            send((0, 0, 0), (0, 0, 1))
            send((0, 0, 0), (0, 1, 0))
            send((0, 0, 0), (0, -1, 0))
            sideways((0, 0, 0))

        def arrive(*steps):
            for step in steps:
                ds, df, dz = step
                landed(buf.at[rows_of(step, rows)], recv_sems.at[index_of(step)], send_sems.at[0])
                if ds == 0:
                    if df == 0:
                        send(step, (0, 1, 0))
                        send(step, (0, -1, 0))
                    elif df == -1 and dz == 0:
                        send(step, (0, 1, 0))
                    elif df == 1 and dz == 1:
                        send(step, (0, -1, 0))
                    sideways(step)
                elif ds == -1 and dz == 0:
                    send(step, (1, 0, 0))
                elif ds == 1 and dz == 1:
                    send(step, (-1, 0, 0))

        return own, arrive

    def kv_put(step, to, half=None):
        where = rows_of(step, SEQ)
        if half is not None:
            where = pl.ds(pl.multiple_of(index_of(step) * SEQ + half * (SEQ // 2), SEQ // 2), SEQ // 2)
        sem = kv_recv.at[2 * CTX if to == (0, 0, 1) else 2 * index_of(step) + (half or 0)]
        push(kv.at[where], kv.at[where], kv_send.at[0], sem, (ctx_of(to), e))

    def kv_arrive(*steps):
        for ds, df, dz in steps:
            at = index_of((ds, df, dz))
            if dz == 0 and (ds == 2 or (ds == 0 and df == 2)):
                for half in (0, 1):
                    where = pl.ds(pl.multiple_of(at * SEQ + half * (SEQ // 2), SEQ // 2), SEQ // 2)
                    landed(kv.at[where], kv_recv.at[2 * at + half], kv_send.at[0])
            elif (ds, df, dz) != (0, 0, 0):
                landed(kv.at[rows_of((ds, df, dz), SEQ)], kv_recv.at[2 * at], kv_send.at[0])
            step = (ds, df, 0)
            if ds == 0:
                if df == 0:
                    kv_put(step, (0, 1, 0))
                    kv_put(step, (0, -1, 0))
                elif df == -1:
                    kv_put(step, (0, 1, 0), 0)
                elif df == 1:
                    kv_put(step, (0, -1, 0), 1)
                kv_put(step, (1, 0, 0))
                kv_put(step, (-1, 0, 0))
            elif ds == -1:
                kv_put(step, (1, 0, 0), 0)
            elif ds == 1:
                kv_put(step, (-1, 0, 0), 1)
            kv_put(step, (0, 0, 1))

    tok_first, tok_arrive = gather(tok, ROWS, tok_send, tok_recv)

    wide[...] = sum(
        taken.astype(F32) * moe_in[r : r + 1, :].astype(F32) for r, (_, taken) in enumerate(slots_of(routes))
    )
    for i in range(EXPERTS):
        slabs[i] = wide[2 * i : 2 * i + 2, :].astype(BF16)

    @pl.loop(1, EXPERTS)
    def _(k):
        to = (e + k) % EXPERTS
        pltpu.make_async_remote_copy(
            src_ref=slabs.at[to], dst_ref=got.at[e], send_sem=go_send.at[0], recv_sem=go_recv.at[0],
            device_id=(c, to), device_id_type=MESH,
        ).start()

    for i in (0, 1):
        kv[rows_of((0, 0, 0), SEQ), i * HEAD : (i + 1) * HEAD] = kv_own[:, i, :]
    kv_arrive((0, 0, 0))

    row = lax.broadcasted_iota(jnp.int32, (SEQ, SEQ), 0)
    col = lax.broadcasted_iota(jnp.int32, (SEQ, SEQ), 1)
    lower = (col <= row).astype(BF16)

    def three(a):
        high = a.astype(BF16)
        mid = (a - high.astype(F32)).astype(BF16)
        low = (a - high.astype(F32) - mid.astype(F32)).astype(BF16)
        return high, mid, low

    cum[...] = sum(dot(lower, term, ((1,), (1,))) for term in three(decay_t[...]))
    cum_t[...] = sum(dot(term, lower, ((1,), (1,))) for term in three(decay_t[...]))
    last = cum[SEQ - 1 : SEQ, :]
    line = lax.broadcasted_iota(jnp.int32, (16, HEAD), 0)
    for h in range(HEADS):
        tail = jnp.exp(last[:, h : h + 1] - cum[:, h : h + 1])
        head = pl.ds(h * HEAD, HEAD)
        scaled = lin_k[:, head].astype(F32) * tail
        state = dot_split(scaled.T, lin_v[:, head])
        high, mid, low = (jnp.broadcast_to(t.astype(F32), (16, HEAD)) for t in three(last[:, h : h + 1]))
        logs = jnp.where(line == 0, high, jnp.where(line == 1, mid, jnp.where(line == 2, low, 0.0))).astype(BF16)
        for i in range(4):
            state_out[4 * h + i, 0:32, :] = state[32 * i : 32 * i + 32].astype(BF16)
            state_out[4 * h + i, 32:48, :] = logs

    @pl.loop(1, CTX)
    def _(k):
        to = (c + k) % CTX
        pltpu.make_async_remote_copy(
            src_ref=state_out.at[to], dst_ref=state_in.at[c], send_sem=st_send.at[0], recv_sem=st_recv.at[0],
            device_id=(to, e), device_id_type=MESH,
        ).start()

    state_in[c] = state_out[c]

    kv_arrive((0, 1, 0), (0, -1, 0))

    got[e] = slabs[e]

    all_of(got.at[pl.ds(0, EXPERTS - 1)], go_send.at[0], go_recv.at[0]).wait()

    for i in range(EXPERTS):
        wide[2 * i : 2 * i + 2, :] = got[i].astype(F32)
    tok[rows_of((0, 0, 0), ROWS), :] = wide[...].astype(BF16)
    tok_first()

    wide_col = lax.broadcasted_iota(jnp.int32, (8, CTX * SEQ), 1)
    blk = jnp.right_shift(wide_col, 7)
    b_s, b_f, b_z = jnp.right_shift(blk, 3), jnp.bitwise_and(jnp.right_shift(blk, 1), 3), jnp.bitwise_and(blk, 1)
    b_ctx = (b_s + core * (b_f - b_s)) * 8 + b_z * 4 + b_f + core * (b_s - b_f)
    place = b_ctx * SEQ + jnp.bitwise_and(wide_col, SEQ - 1)
    line8 = lax.broadcasted_iota(jnp.int32, (8, CTX * SEQ), 0)

    @pl.loop(0, SEQ // 8)
    def _(i):
        bias[pl.ds(pl.multiple_of(i * 8, 8), 8), :] = jnp.where(place <= c * SEQ + i * 8 + line8, 0.0, -1e30)

    def attend(first, count):
        @pl.loop(first, first + count)
        def _(h):
            head = pl.ds(pl.multiple_of(h * HEAD, HEAD), HEAD)
            scores = dot(soft_q[:, head], kv[:, 0:HEAD], ((1,), (1,))) * SCALE + bias[...]
            top = jnp.max(scores, axis=1, keepdims=True)
            probs = jnp.exp(scores - top)
            total = jnp.sum(probs, axis=1, keepdims=True)
            mixed = dot(probs.astype(BF16), kv[:, HEAD : 2 * HEAD])
            soft_out[:, head] = (mixed / total).astype(BF16)

    def finish_lightning(heads):
        for h in heads:
            head = pl.ds(h * HEAD, HEAD)
            here = cum[:, h : h + 1]
            spread = here - cum_t[h : h + 1, :]
            decays = jnp.where(col <= row, jnp.exp(jnp.where(col <= row, spread, 0.0)), 0.0)
            scores = dot(lin_q[:, head], lin_k[:, head], ((1,), (1,))) * SCALE
            within = dot_split(scores * decays, lin_v[:, head])
            before = prior[4 * h : 4 * h + 4].reshape(HEAD, HEAD)
            combined = within + jnp.exp(here) * dot(lin_q[:, head], before) * SCALE
            root = jnp.sqrt(jnp.mean(combined * combined, axis=1, keepdims=True) + 1e-06)
            lin_out[:, head] = (combined / root * gain[:, head]).astype(BF16)

    chunk = 1024

    def group(ds):
        return pl.ds(pl.multiple_of((s + ds + 4) % 4 * 8 * ROWS, 8 * ROWS), 8 * ROWS)

    def enter(ds):
        def add(k, sums):
            at = pl.ds(pl.multiple_of(k * chunk, chunk), chunk)
            tokens = tok[group(ds), at]
            return (
                sums[0] + dot(tokens, gate[:, at], ((1,), (1,))),
                sums[1] + dot(tokens, up[:, at], ((1,), (1,))),
            )

        zero = jnp.zeros((8 * ROWS, FF), F32)
        a, b = lax.fori_loop(0, D // chunk, add, (zero, zero))
        hidden[group(ds), :] = (a / (1.0 + jnp.exp(-a)) * b).astype(BF16)

    def leave(ds):
        @pl.loop(0, D // chunk)
        def _(k):
            at = pl.ds(pl.multiple_of(k * chunk, chunk), chunk)
            part[group(ds), at] = dot(hidden[group(ds), :], down[:, at]).astype(BF16)

    def pairs(df, dz):
        return (1, df, dz), (-1, df, dz)

    kv_arrive(*pairs(0, 0), (0, 2, 0))
    tok_arrive((0, 0, 1), (0, 1, 0), (0, -1, 0))
    kv_arrive(*pairs(1, 0), *pairs(-1, 0))
    tok_arrive(*pairs(0, 0))
    kv_arrive(*pairs(2, 0))
    tok_arrive((0, 1, 1), (0, -1, 1))
    kv_arrive((2, 0, 0), (2, 1, 0))
    tok_arrive(*pairs(0, 1), (0, 2, 0), (0, 2, 1))
    kv_arrive((2, -1, 0), (2, 2, 0))
    tok_arrive(*pairs(1, 0), *pairs(-1, 0))
    tok_arrive(*pairs(1, 1), *pairs(-1, 1))
    for copy in weights:
        copy.wait()
    enter(0)
    tok_arrive(*pairs(2, 0), *pairs(2, 1))
    enter(1)
    enter(-1)
    landed(kv.at[pl.ds(0, CTX // 2 * SEQ)], kv_recv.at[2 * CTX], kv_send.at[0])

    all_of(state_in.at[pl.ds(0, CTX - 1)], st_send.at[0], st_recv.at[0]).wait()

    def hop(i, run):
        prior_out[i] = run.astype(BF16)
        logs = jnp.sum(state_in[i, 32:48, :].astype(F32), axis=0, keepdims=True)
        return jnp.exp(logs) * run + state_in[i, 0:32, :].astype(F32)

    lax.fori_loop(0, CTX, hop, jnp.zeros((32, HEAD), F32))

    @pl.loop(1, CTX)
    def _(k):
        to = (c + k) % CTX
        pltpu.make_async_remote_copy(
            src_ref=prior_out.at[to], dst_ref=prior.at[c], send_sem=pr_send.at[0], recv_sem=pr_recv.at[0],
            device_id=(to, e), device_id_type=MESH,
        ).start()

    prior[c] = prior_out[c]

    tok_arrive(*((2, df, dz) for df in (0, 1, -1, 2) for dz in (0, 1)))
    enter(2)

    numbered = tuple(enumerate(DFS))

    def put(src, dst, kind, sem, to):
        push(src, dst, rs_send.at[kind], sem, (ctx_of(to), e))

    def piece(side, step):
        ds, df, unit = step
        if side:
            return part.at[rows_of((ds, df, 0), ROWS), pl.ds(MAIN + SIDE * unit, SIDE)]
        return part.at[rows_of(step, ROWS), pl.ds(0, MAIN)]

    def block(ref, side, i):
        return ref.at[pl.ds(i * ROWS, ROWS), pl.ds(MAIN, SIDE) if side else pl.ds(0, MAIN)]

    def add_in(ref, *blocks):
        total = ref[...].astype(F32)
        for b in blocks:
            total = total + b[...].astype(F32)
        ref[...] = total.astype(BF16)

    def take(ref, sems, side, count, i):
        landed(block(ref, side, i), sems.at[side * count + i], rs_send.at[0])
        return block(ref, side, i)

    def over(side, step, ref, sems, count, i, to):
        put(piece(side, step), block(ref, side, i), side, sems.at[side * count + i], to)

    def z_rest(i):
        return zt.at[pl.ds(i * ROWS, ROWS)]

    def z_send(ds):
        for i, df in numbered:
            at = 4 * DFS.index(ds) + i
            src = part.at[rows_of((ds, df, 1), ROWS), pl.ds(MAIN, 2 * SIDE)]
            put(src, z_rest(at), 2, z_sem.at[1 + at], (0, 0, 1))

    def z_add(ds, df):
        at = 4 * DFS.index(ds) + DFS.index(df)
        landed(z_rest(at), z_sem.at[1 + at], rs_send.at[0])
        add_in(part.at[rows_of((ds, df, 0), ROWS), pl.ds(MAIN, 2 * SIDE)], z_rest(at))

    def first(side, i, df):
        over(side, (2, df, 0), s1r, s1_sem, 8, 2 * i, (-1, 0, 0))
        over(side, (2, df, 1), s1r, s1_sem, 8, 2 * i + 1, (1, 0, 0))

    def own_minus(side, i, df):
        over(side, (-1, df, 1), s2r, s2_sem, 16, 4 * i + 1, (-1, 0, 0))

    def own_plus(side, i, df):
        over(side, (1, df, 0), s2r, s2_sem, 16, 4 * i + 2, (1, 0, 0))

    def forward(side, i, df):
        for unit, ds in ((0, -1), (1, 1)):
            add_in(piece(side, (ds, df, unit)), take(s1r, s1_sem, side, 8, 2 * i + unit))
            over(side, (ds, df, unit), s2r, s2_sem, 16, 4 * i + 3 * unit, (ds, 0, 0))

    def settle(side, i, df):
        got_s = [take(s2r, s2_sem, side, 16, 4 * i + k) for k in (1, 2, 0, 3)]
        add_in(piece(side, (0, df, 0)), got_s[2], got_s[1])
        add_in(piece(side, (0, df, 1)), got_s[0], got_s[3])
        if df == 2:
            over(side, (0, 2, 0), f1r, f1_sem, 2, 0, (0, -1, 0))
            over(side, (0, 2, 1), f1r, f1_sem, 2, 1, (0, 1, 0))
        elif df == 1:
            over(side, (0, 1, 0), f2r, f2_sem, 4, 2, (0, 1, 0))
        elif df == -1:
            over(side, (0, -1, 1), f2r, f2_sem, 4, 1, (0, -1, 0))
            for unit, way in ((0, -1), (1, 1)):
                add_in(piece(side, (0, way, unit)), take(f1r, f1_sem, side, 2, unit))
                over(side, (0, way, unit), f2r, f2_sem, 4, 3 * unit, (0, way, 0))

    def total(side, unit):
        here = [take(f2r, f2_sem, side, 4, k) for k in (unit, 2 + unit)]
        return piece(side, (0, 0, unit))[...].astype(F32) + here[0][...].astype(F32) + here[1][...].astype(F32)

    leave(2)
    z_send(2)
    for i, df in numbered:
        first(0, i, df)
    leave(-1)
    z_send(-1)
    for i, df in numbered:
        own_minus(0, i, df)
    leave(1)
    z_send(1)
    for i, df in numbered:
        own_plus(0, i, df)
    leave(0)
    z_send(0)

    all_of(prior.at[pl.ds(0, CTX - 1)], pr_send.at[0], pr_recv.at[0]).wait()

    for i, df in numbered:
        forward(0, i, df)
        z_add(2, df)
        first(1, i, df)
        attend(2 * i, 2)
        finish_lightning((2 * i, 2 * i + 1))
    settle(0, 0, 2)
    for i, df in numbered:
        z_add(-1, df)
        own_minus(1, i, df)
    settle(0, 1, 1)
    for i, df in numbered:
        z_add(1, df)
        own_plus(1, i, df)
        forward(1, i, df)
    settle(0, 2, -1)
    z_add(0, 2)
    settle(1, 0, 2)
    settle(0, 3, 0)
    for i, df in numbered[1:3]:
        z_add(0, df)
        settle(1, i, df)
    piece(0, (0, 0, 1))[...] = total(0, 1).astype(BF16)
    put(piece(0, (0, 0, 1)), zr, 0, z_sem.at[0], (0, 0, 1))
    wide[:, pl.ds(0, MAIN)] = total(0, 0)
    z_add(0, 0)
    settle(1, 3, 0)
    for unit in (0, 1):
        wide[:, pl.ds(MAIN + SIDE * unit, SIDE)] = total(1, unit)
    landed(zr, z_sem.at[0], rs_send.at[0])
    wide[:, pl.ds(0, MAIN)] = wide[:, pl.ds(0, MAIN)] + zr[...].astype(F32)

    for i in range(EXPERTS):
        back[i] = wide[2 * i : 2 * i + 2, :].astype(BF16)

    @pl.loop(1, EXPERTS)
    def _(k):
        to = (e + k) % EXPERTS
        pltpu.make_async_remote_copy(
            src_ref=back.at[to], dst_ref=ret.at[e], send_sem=back_send.at[0], recv_sem=back_recv.at[0],
            device_id=(c, to), device_id_type=MESH,
        ).start()

    ret[e] = back[e]

    all_of(back.at[pl.ds(0, EXPERTS - 1)], back_send.at[0], back_recv.at[0]).wait()

    all_of(tok.at[pl.ds(0, 31 * ROWS)], tok_send.at[0], tok_recv.at[0]).wait_send()
    all_of(kv.at[pl.ds(0, 26 * SEQ + 10 * SEQ // 2)], kv_send.at[0], kv_recv.at[0]).wait_send()
    for kind, blocks, columns in ((0, 31, MAIN), (1, 30, SIDE), (2, 16, 2 * SIDE)):
        sent = part.at[pl.ds(0, blocks * ROWS), pl.ds(0, columns)]
        all_of(sent, rs_send.at[kind], z_sem.at[0]).wait_send()


def on_device(
    lin_query,
    lin_key,
    lin_value,
    log_decay,
    lin_gain,
    moe_input,
    routes,
    route_weight,
    gate_weight,
    up_weight,
    down_weight,
    soft_query,
    soft_kv,
):
    vmem, any_ = pl.BlockSpec(memory_space=pltpu.VMEM), pl.BlockSpec(memory_space=pl.ANY)
    smem = pl.BlockSpec(memory_space=pltpu.SMEM)
    dma = pltpu.SemaphoreType.DMA
    ret, lin, soft = pl.pallas_call(
        kernel,
        out_shape=(
            jax.ShapeDtypeStruct((EXPERTS, CAP, D), BF16),
            jax.ShapeDtypeStruct((SEQ, HEADS * HEAD), BF16),
            jax.ShapeDtypeStruct((SEQ, HEADS * HEAD), BF16),
        ),
        in_specs=[smem, vmem, vmem, any_, any_, any_] + [vmem] * 6,
        out_specs=(vmem, vmem, vmem),
        scratch_shapes=[
            pltpu.VMEM((CTX * SEQ, 2 * HEAD), BF16),
            pltpu.VMEM((CTX * ROWS, D), BF16),
            pltpu.VMEM((CTX * ROWS, D), BF16),
            pltpu.VMEM((8 * ROWS, D), BF16),
            pltpu.VMEM((16 * ROWS, D), BF16),
            pltpu.VMEM((2 * ROWS, D), BF16),
            pltpu.VMEM((4 * ROWS, D), BF16),
            pltpu.VMEM((ROWS, MAIN), BF16),
            pltpu.VMEM((16 * ROWS, 2 * SIDE), BF16),
            pltpu.VMEM((EXPERTS, CAP, D), BF16),
            pltpu.VMEM((EXPERTS, CAP, D), BF16),
            pltpu.VMEM((EXPERTS, CAP, D), BF16),
            pltpu.VMEM((ROWS, D), F32),
            pltpu.VMEM((FF, D), BF16),
            pltpu.VMEM((FF, D), BF16),
            pltpu.VMEM((FF, D), BF16),
            pltpu.VMEM((CTX * ROWS, FF), BF16),
            pltpu.VMEM((SEQ, CTX * SEQ), F32),
            pltpu.VMEM((SEQ, HEADS), F32),
            pltpu.VMEM((HEADS, SEQ), F32),
            pltpu.VMEM((CTX, 48, HEAD), BF16),
            pltpu.VMEM((CTX, 48, HEAD), BF16),
            pltpu.VMEM((CTX, 32, HEAD), BF16),
            pltpu.VMEM((CTX, 32, HEAD), BF16),
            dma((3,)),
            dma((1,)), dma((2 * CTX + 1,)), dma((1,)), dma((CTX,)), dma((3,)),
            dma((16,)), dma((32,)), dma((4,)), dma((8,)), dma((17,)),
            dma((1,)), dma((1,)), dma((1,)), dma((1,)),
            dma((1,)), dma((1,)), dma((1,)), dma((1,)),
        ],
        compiler_params=pltpu.CompilerParams(
            collective_id=0, has_side_effects=True, vmem_limit_bytes=58 * 2**20
        ),
    )(
        routes.T,
        moe_input,
        soft_kv.reshape(SEQ, 2, HEAD),
        gate_weight.reshape(D, FF).T,
        up_weight.reshape(D, FF).T,
        down_weight.reshape(FF, D),
        lin_query,
        lin_key,
        lin_value,
        log_decay.T,
        lin_gain.reshape(1, HEADS * HEAD),
        soft_query,
    )
    lin_out, moe_out, soft_out = pl.pallas_call(
        finish,
        out_shape=(
            jax.ShapeDtypeStruct((SEQ, HEADS * HEAD), BF16),
            jax.ShapeDtypeStruct(moe_input.shape, BF16),
            jax.ShapeDtypeStruct((SEQ, HEADS * HEAD), BF16),
        ),
        in_specs=[smem, smem, vmem, vmem, vmem],
        out_specs=(vmem, vmem, vmem),
        scratch_shapes=[pltpu.VMEM((ROWS, D), F32)],
    )(routes.T, route_weight.T, ret, lin, soft)
    return (lin_out, moe_out, soft_out)


def solution(mesh):
    placed = (
        P("ctx", "exp"),
        P("ctx", "exp"),
        P("ctx", "exp"),
        P("ctx", "exp"),
        P("exp"),
        P(("ctx", "exp"), None),
        P(("ctx", "exp"), None),
        P(("ctx", "exp"), None),
        P("exp", None, "ctx"),
        P("exp", None, "ctx"),
        P("exp", "ctx", None),
        P("ctx", "exp"),
        P("ctx", "exp", None, None),
    )
    return jax.shard_map(
        on_device,
        mesh=mesh,
        in_specs=placed,
        out_specs=(P("ctx", "exp"), P(("ctx", "exp"), None), P("ctx", "exp")),
        check_vma=False,
    )
```

```python
import math

import jax
import jax.numpy as jnp
from jax import lax
from jax.experimental import pallas as pl
from jax.experimental.pallas import tpu as pltpu
from jax.sharding import PartitionSpec as P

D = 6144
HEAD = 128
EXPERTS = 8
TOP = 2
CAP = 2
CTX = 32
SEQ = 128
HEADS = 8
FF = 288
ROWS = 16
SCALE = 1.0 / math.sqrt(HEAD)
F32, BF16 = jnp.float32, jnp.bfloat16
MESH = pl.DeviceIdType.MESH
DFS = (2, 1, -1, 0)
MAIN, SIDE = 3584, 1280


def dot(a, b, dims=((1,), (0,))):
    return lax.dot_general(a, b, (dims, ((), ())), preferred_element_type=F32)


def dot_split(a, b, dims=((1,), (0,))):
    high = a.astype(BF16)
    low = (a - high.astype(F32)).astype(BF16)
    return dot(high, b, dims) + dot(low, b, dims)


def slots_of(routes):
    line = lax.broadcasted_iota(jnp.int32, (ROWS, 1), 0)
    expert, place = jnp.right_shift(line, 1), jnp.bitwise_and(line, 1)
    met = jnp.zeros((ROWS, 1), jnp.int32)
    found = []
    for r in range(6):
        named = (expert == routes[0, r]) | (expert == routes[1, r])
        found.append((expert, named & (met == place)))
        met = met + named.astype(jnp.int32)
    return found


def finish(routes, weights, ret, lin, soft, lin_out, moe_out, soft_out, wide):
    lin_out[...] = lin[...]
    soft_out[...] = soft[...]
    for i in range(EXPERTS):
        wide[2 * i : 2 * i + 2, :] = ret[i].astype(F32)
    for r, (expert, taken) in enumerate(slots_of(routes)):
        weight = jnp.where(expert == routes[0, r], weights[0, r], weights[1, r])
        mixed = jnp.sum(jnp.where(taken, weight, 0.0) * wide[...], axis=0, keepdims=True)
        moe_out[r : r + 1, :] = mixed.astype(BF16)


def kernel(
    routes, moe_in, kv_own, gate_hbm, up_hbm, down_hbm, lin_q, lin_k, lin_v, decay_t, gain, soft_q,
    ret, lin_out, soft_out,
    kv, tok, part, s1r, s2r, f1r, f2r, zr, zt, slabs, got, back, wide, gate, up, down, hidden,
    bias, cum, cum_t, state_out, state_in, prior_out, prior,
    w_sem, kv_send, kv_recv, tok_send, tok_recv, rs_send, s1_sem, s2_sem, f1_sem, f2_sem, z_sem,
    go_send, go_recv, back_send, back_recv, st_send, st_recv, pr_send, pr_recv,
):
    c, e = lax.axis_index("ctx"), lax.axis_index("exp")
    y, z, x, core = c // 8, (c // 4) % 2, c % 4, e % 2
    f, s = x + core * (y - x), y + core * (x - y)

    def rel(step):
        ds, df, dz = step
        return (s + ds + 4) % 4, (f + df + 4) % 4, (z + dz) % 2

    def ctx_of(step):
        ss, ff, zz = rel(step)
        return (ss + core * (ff - ss)) * 8 + zz * 4 + ff + core * (ss - ff)

    def index_of(step):
        ss, ff, zz = rel(step)
        return ss * 8 + ff * 2 + zz

    def rows_of(step, rows):
        return pl.ds(pl.multiple_of(index_of(step) * rows, rows), rows)

    barrier = pltpu.get_barrier_semaphore()

    @pl.loop(1, CTX)
    def _(k):
        pl.semaphore_signal(barrier, inc=1, device_id=((c + k) % CTX, e), device_id_type=MESH)

    @pl.loop(1, EXPERTS)
    def _(k):
        pl.semaphore_signal(barrier, inc=1, device_id=(c, (e + k) % EXPERTS), device_id_type=MESH)

    pl.semaphore_wait(barrier, CTX - 1 + EXPERTS - 1)

    weights = [
        pltpu.make_async_copy(src, dst, w_sem.at[i])
        for i, (src, dst) in enumerate(((gate_hbm, gate), (up_hbm, up), (down_hbm, down)))
    ]
    for copy in weights:
        copy.start()

    def push(src, dst, send_sem, recv_sem, to):
        pltpu.make_async_remote_copy(
            src_ref=src, dst_ref=dst, send_sem=send_sem, recv_sem=recv_sem, device_id=to, device_id_type=MESH
        ).start()

    def landed(ref, recv_sem, spare_sem):
        pltpu.make_async_remote_copy(
            src_ref=ref, dst_ref=ref, send_sem=spare_sem, recv_sem=recv_sem,
            device_id=(ctx_of((0, 0, 1)), e), device_id_type=MESH,
        ).wait_recv()

    def all_of(ref, send_sem, recv_sem):
        return pltpu.make_async_remote_copy(
            src_ref=ref, dst_ref=ref, send_sem=send_sem, recv_sem=recv_sem,
            device_id=(ctx_of((0, 0, 1)), e), device_id_type=MESH,
        )

    def gather(buf, rows, send_sems, recv_sems):
        def send(step, to):
            where = rows_of(step, rows)
            push(buf.at[where], buf.at[where], send_sems.at[0], recv_sems.at[index_of(step)], (ctx_of(to), e))

        def sideways(step):
            send(step, (1, 0, 0))
            send(step, (-1, 0, 0))

        def own():
            send((0, 0, 0), (0, 0, 1))
            send((0, 0, 0), (0, 1, 0))
            send((0, 0, 0), (0, -1, 0))
            sideways((0, 0, 0))

        def arrive(*steps):
            for step in steps:
                ds, df, dz = step
                landed(buf.at[rows_of(step, rows)], recv_sems.at[index_of(step)], send_sems.at[0])
                if ds == 0:
                    if df == 0:
                        send(step, (0, 1, 0))
                        send(step, (0, -1, 0))
                    elif df == -1 and dz == 0:
                        send(step, (0, 1, 0))
                    elif df == 1 and dz == 1:
                        send(step, (0, -1, 0))
                    sideways(step)
                elif ds == -1 and dz == 0:
                    send(step, (1, 0, 0))
                elif ds == 1 and dz == 1:
                    send(step, (-1, 0, 0))

        return own, arrive

    def kv_put(step, to, half=None):
        where = rows_of(step, SEQ)
        if half is not None:
            where = pl.ds(pl.multiple_of(index_of(step) * SEQ + half * (SEQ // 2), SEQ // 2), SEQ // 2)
        sem = kv_recv.at[2 * CTX if to == (0, 0, 1) else 2 * index_of(step) + (half or 0)]
        push(kv.at[where], kv.at[where], kv_send.at[0], sem, (ctx_of(to), e))

    def kv_arrive(*steps):
        for ds, df, dz in steps:
            at = index_of((ds, df, dz))
            if dz == 0 and (ds == 2 or (ds == 0 and df == 2)):
                for half in (0, 1):
                    where = pl.ds(pl.multiple_of(at * SEQ + half * (SEQ // 2), SEQ // 2), SEQ // 2)
                    landed(kv.at[where], kv_recv.at[2 * at + half], kv_send.at[0])
            elif (ds, df, dz) != (0, 0, 0):
                landed(kv.at[rows_of((ds, df, dz), SEQ)], kv_recv.at[2 * at], kv_send.at[0])
            step = (ds, df, 0)
            if ds == 0:
                if df == 0:
                    kv_put(step, (0, 1, 0))
                    kv_put(step, (0, -1, 0))
                elif df == -1:
                    kv_put(step, (0, 1, 0), 0)
                elif df == 1:
                    kv_put(step, (0, -1, 0), 1)
                kv_put(step, (1, 0, 0))
                kv_put(step, (-1, 0, 0))
            elif ds == -1:
                kv_put(step, (1, 0, 0), 0)
            elif ds == 1:
                kv_put(step, (-1, 0, 0), 1)
            kv_put(step, (0, 0, 1))

    tok_first, tok_arrive = gather(tok, ROWS, tok_send, tok_recv)

    wide[...] = sum(
        taken.astype(F32) * moe_in[r : r + 1, :].astype(F32) for r, (_, taken) in enumerate(slots_of(routes))
    )
    for i in range(EXPERTS):
        slabs[i] = wide[2 * i : 2 * i + 2, :].astype(BF16)

    @pl.loop(1, EXPERTS)
    def _(k):
        to = (e + k) % EXPERTS
        pltpu.make_async_remote_copy(
            src_ref=slabs.at[to], dst_ref=got.at[e], send_sem=go_send.at[0], recv_sem=go_recv.at[0],
            device_id=(c, to), device_id_type=MESH,
        ).start()

    for i in (0, 1):
        kv[rows_of((0, 0, 0), SEQ), i * HEAD : (i + 1) * HEAD] = kv_own[:, i, :]
    kv_arrive((0, 0, 0))

    row = lax.broadcasted_iota(jnp.int32, (SEQ, SEQ), 0)
    col = lax.broadcasted_iota(jnp.int32, (SEQ, SEQ), 1)
    lower = (col <= row).astype(BF16)

    def three(a):
        high = a.astype(BF16)
        mid = (a - high.astype(F32)).astype(BF16)
        low = (a - high.astype(F32) - mid.astype(F32)).astype(BF16)
        return high, mid, low

    cum[...] = sum(dot(lower, term, ((1,), (1,))) for term in three(decay_t[...]))
    cum_t[...] = sum(dot(term, lower, ((1,), (1,))) for term in three(decay_t[...]))
    last = cum[SEQ - 1 : SEQ, :]
    line = lax.broadcasted_iota(jnp.int32, (16, HEAD), 0)
    for h in range(HEADS):
        tail = jnp.exp(last[:, h : h + 1] - cum[:, h : h + 1])
        head = pl.ds(h * HEAD, HEAD)
        scaled = lin_k[:, head].astype(F32) * tail
        state = dot_split(scaled.T, lin_v[:, head])
        high, mid, low = (jnp.broadcast_to(t.astype(F32), (16, HEAD)) for t in three(last[:, h : h + 1]))
        logs = jnp.where(line == 0, high, jnp.where(line == 1, mid, jnp.where(line == 2, low, 0.0))).astype(BF16)
        for i in range(4):
            state_out[4 * h + i, 0:32, :] = state[32 * i : 32 * i + 32].astype(BF16)
            state_out[4 * h + i, 32:48, :] = logs

    @pl.loop(1, CTX)
    def _(k):
        to = (c + k) % CTX
        pltpu.make_async_remote_copy(
            src_ref=state_out.at[to], dst_ref=state_in.at[c], send_sem=st_send.at[0], recv_sem=st_recv.at[0],
            device_id=(to, e), device_id_type=MESH,
        ).start()

    state_in[c] = state_out[c]

    kv_arrive((0, 1, 0), (0, -1, 0))

    got[e] = slabs[e]

    all_of(got.at[pl.ds(0, EXPERTS - 1)], go_send.at[0], go_recv.at[0]).wait()

    for i in range(EXPERTS):
        wide[2 * i : 2 * i + 2, :] = got[i].astype(F32)
    tok[rows_of((0, 0, 0), ROWS), :] = wide[...].astype(BF16)
    tok_first()

    wide_col = lax.broadcasted_iota(jnp.int32, (8, CTX * SEQ), 1)
    blk = jnp.right_shift(wide_col, 7)
    b_s, b_f, b_z = jnp.right_shift(blk, 3), jnp.bitwise_and(jnp.right_shift(blk, 1), 3), jnp.bitwise_and(blk, 1)
    b_ctx = (b_s + core * (b_f - b_s)) * 8 + b_z * 4 + b_f + core * (b_s - b_f)
    place = b_ctx * SEQ + jnp.bitwise_and(wide_col, SEQ - 1)
    line8 = lax.broadcasted_iota(jnp.int32, (8, CTX * SEQ), 0)

    @pl.loop(0, SEQ // 8)
    def _(i):
        bias[pl.ds(pl.multiple_of(i * 8, 8), 8), :] = jnp.where(place <= c * SEQ + i * 8 + line8, 0.0, -1e30)

    def attend(first, count):
        @pl.loop(first, first + count)
        def _(h):
            head = pl.ds(pl.multiple_of(h * HEAD, HEAD), HEAD)
            scores = dot(soft_q[:, head], kv[:, 0:HEAD], ((1,), (1,))) * SCALE + bias[...]
            top = jnp.max(scores, axis=1, keepdims=True)
            probs = jnp.exp(scores - top)
            total = jnp.sum(probs, axis=1, keepdims=True)
            mixed = dot(probs.astype(BF16), kv[:, HEAD : 2 * HEAD])
            soft_out[:, head] = (mixed / total).astype(BF16)

    def finish_lightning(heads):
        for h in heads:
            head = pl.ds(h * HEAD, HEAD)
            here = cum[:, h : h + 1]
            spread = here - cum_t[h : h + 1, :]
            decays = jnp.where(col <= row, jnp.exp(jnp.where(col <= row, spread, 0.0)), 0.0)
            scores = dot(lin_q[:, head], lin_k[:, head], ((1,), (1,))) * SCALE
            within = dot_split(scores * decays, lin_v[:, head])
            before = prior[4 * h : 4 * h + 4].reshape(HEAD, HEAD)
            combined = within + jnp.exp(here) * dot(lin_q[:, head], before) * SCALE
            root = jnp.sqrt(jnp.mean(combined * combined, axis=1, keepdims=True) + 1e-06)
            lin_out[:, head] = (combined / root * gain[:, head]).astype(BF16)

    chunk = 1024

    def group(ds):
        return pl.ds(pl.multiple_of((s + ds + 4) % 4 * 8 * ROWS, 8 * ROWS), 8 * ROWS)

    def enter(ds):
        def add(k, sums):
            at = pl.ds(pl.multiple_of(k * chunk, chunk), chunk)
            tokens = tok[group(ds), at]
            return (
                sums[0] + dot(tokens, gate[:, at], ((1,), (1,))),
                sums[1] + dot(tokens, up[:, at], ((1,), (1,))),
            )

        zero = jnp.zeros((8 * ROWS, FF), F32)
        a, b = lax.fori_loop(0, D // chunk, add, (zero, zero))
        hidden[group(ds), :] = (a / (1.0 + jnp.exp(-a)) * b).astype(BF16)

    def leave(ds):
        @pl.loop(0, D // chunk)
        def _(k):
            at = pl.ds(pl.multiple_of(k * chunk, chunk), chunk)
            part[group(ds), at] = dot(hidden[group(ds), :], down[:, at]).astype(BF16)

    def pairs(df, dz):
        return (1, df, dz), (-1, df, dz)

    kv_arrive(*pairs(0, 0), (0, 2, 0))
    tok_arrive((0, 0, 1), (0, 1, 0), (0, -1, 0))
    kv_arrive(*pairs(1, 0), *pairs(-1, 0))
    tok_arrive(*pairs(0, 0))
    kv_arrive(*pairs(2, 0))
    tok_arrive((0, 1, 1), (0, -1, 1))
    kv_arrive((2, 0, 0), (2, 1, 0))
    tok_arrive(*pairs(0, 1), (0, 2, 0), (0, 2, 1))
    kv_arrive((2, -1, 0), (2, 2, 0))
    tok_arrive(*pairs(1, 0), *pairs(-1, 0))
    tok_arrive(*pairs(1, 1), *pairs(-1, 1))
    for copy in weights:
        copy.wait()
    enter(0)
    all_of(state_in.at[pl.ds(0, CTX - 1)], st_send.at[0], st_recv.at[0]).wait()

    def hop(i, run):
        prior_out[i] = run.astype(BF16)
        logs = jnp.sum(state_in[i, 32:48, :].astype(F32), axis=0, keepdims=True)
        return jnp.exp(logs) * run + state_in[i, 0:32, :].astype(F32)

    lax.fori_loop(0, CTX, hop, jnp.zeros((32, HEAD), F32))

    @pl.loop(1, CTX)
    def _(k):
        to = (c + k) % CTX
        pltpu.make_async_remote_copy(
            src_ref=prior_out.at[to], dst_ref=prior.at[c], send_sem=pr_send.at[0], recv_sem=pr_recv.at[0],
            device_id=(to, e), device_id_type=MESH,
        ).start()

    prior[c] = prior_out[c]
    tok_arrive(*pairs(2, 0), *pairs(2, 1))
    enter(1)
    enter(-1)
    landed(kv.at[pl.ds(0, CTX // 2 * SEQ)], kv_recv.at[2 * CTX], kv_send.at[0])

    tok_arrive(*((2, df, dz) for df in (0, 1, -1, 2) for dz in (0, 1)))
    enter(2)

    numbered = tuple(enumerate(DFS))

    def put(src, dst, kind, sem, to):
        push(src, dst, rs_send.at[kind], sem, (ctx_of(to), e))

    def piece(side, step):
        ds, df, unit = step
        if side:
            return part.at[rows_of((ds, df, 0), ROWS), pl.ds(MAIN + SIDE * unit, SIDE)]
        return part.at[rows_of(step, ROWS), pl.ds(0, MAIN)]

    def block(ref, side, i):
        return ref.at[pl.ds(i * ROWS, ROWS), pl.ds(MAIN, SIDE) if side else pl.ds(0, MAIN)]

    def add_in(ref, *blocks):
        total = ref[...].astype(F32)
        for b in blocks:
            total = total + b[...].astype(F32)
        ref[...] = total.astype(BF16)

    def take(ref, sems, side, count, i):
        landed(block(ref, side, i), sems.at[side * count + i], rs_send.at[0])
        return block(ref, side, i)

    def over(side, step, ref, sems, count, i, to):
        put(piece(side, step), block(ref, side, i), side, sems.at[side * count + i], to)

    def z_rest(i):
        return zt.at[pl.ds(i * ROWS, ROWS)]

    def z_send(ds):
        for i, df in numbered:
            at = 4 * DFS.index(ds) + i
            src = part.at[rows_of((ds, df, 1), ROWS), pl.ds(MAIN, 2 * SIDE)]
            put(src, z_rest(at), 2, z_sem.at[1 + at], (0, 0, 1))

    def z_add(ds, df):
        at = 4 * DFS.index(ds) + DFS.index(df)
        landed(z_rest(at), z_sem.at[1 + at], rs_send.at[0])
        add_in(part.at[rows_of((ds, df, 0), ROWS), pl.ds(MAIN, 2 * SIDE)], z_rest(at))

    def first(side, i, df):
        over(side, (2, df, 0), s1r, s1_sem, 8, 2 * i, (-1, 0, 0))
        over(side, (2, df, 1), s1r, s1_sem, 8, 2 * i + 1, (1, 0, 0))

    def own_minus(side, i, df):
        over(side, (-1, df, 1), s2r, s2_sem, 16, 4 * i + 1, (-1, 0, 0))

    def own_plus(side, i, df):
        over(side, (1, df, 0), s2r, s2_sem, 16, 4 * i + 2, (1, 0, 0))

    def forward(side, i, df):
        for unit, ds in ((0, -1), (1, 1)):
            add_in(piece(side, (ds, df, unit)), take(s1r, s1_sem, side, 8, 2 * i + unit))
            over(side, (ds, df, unit), s2r, s2_sem, 16, 4 * i + 3 * unit, (ds, 0, 0))

    def settle(side, i, df):
        got_s = [take(s2r, s2_sem, side, 16, 4 * i + k) for k in (1, 2, 0, 3)]
        add_in(piece(side, (0, df, 0)), got_s[2], got_s[1])
        add_in(piece(side, (0, df, 1)), got_s[0], got_s[3])
        if df == 2:
            over(side, (0, 2, 0), f1r, f1_sem, 2, 0, (0, -1, 0))
            over(side, (0, 2, 1), f1r, f1_sem, 2, 1, (0, 1, 0))
        elif df == 1:
            over(side, (0, 1, 0), f2r, f2_sem, 4, 2, (0, 1, 0))
        elif df == -1:
            over(side, (0, -1, 1), f2r, f2_sem, 4, 1, (0, -1, 0))
            for unit, way in ((0, -1), (1, 1)):
                add_in(piece(side, (0, way, unit)), take(f1r, f1_sem, side, 2, unit))
                over(side, (0, way, unit), f2r, f2_sem, 4, 3 * unit, (0, way, 0))

    def total(side, unit):
        here = [take(f2r, f2_sem, side, 4, k) for k in (unit, 2 + unit)]
        return piece(side, (0, 0, unit))[...].astype(F32) + here[0][...].astype(F32) + here[1][...].astype(F32)

    leave(2)
    z_send(2)
    for i, df in numbered:
        first(0, i, df)
    leave(-1)
    z_send(-1)
    for i, df in numbered:
        own_minus(0, i, df)
    leave(1)
    z_send(1)
    for i, df in numbered:
        own_plus(0, i, df)
    leave(0)
    z_send(0)

    all_of(prior.at[pl.ds(0, CTX - 1)], pr_send.at[0], pr_recv.at[0]).wait()

    for i, df in numbered:
        forward(0, i, df)
        z_add(2, df)
        first(1, i, df)
        attend(2 * i, 2)
        finish_lightning((2 * i, 2 * i + 1))
    settle(0, 0, 2)
    for i, df in numbered:
        z_add(-1, df)
        own_minus(1, i, df)
    settle(0, 1, 1)
    for i, df in numbered:
        z_add(1, df)
        own_plus(1, i, df)
        forward(1, i, df)
    settle(0, 2, -1)
    z_add(0, 2)
    settle(1, 0, 2)
    settle(0, 3, 0)
    for i, df in numbered[1:3]:
        z_add(0, df)
        settle(1, i, df)
    piece(0, (0, 0, 1))[...] = total(0, 1).astype(BF16)
    put(piece(0, (0, 0, 1)), zr, 0, z_sem.at[0], (0, 0, 1))
    wide[:, pl.ds(0, MAIN)] = total(0, 0)
    z_add(0, 0)
    settle(1, 3, 0)
    for unit in (0, 1):
        wide[:, pl.ds(MAIN + SIDE * unit, SIDE)] = total(1, unit)
    landed(zr, z_sem.at[0], rs_send.at[0])
    wide[:, pl.ds(0, MAIN)] = wide[:, pl.ds(0, MAIN)] + zr[...].astype(F32)

    for i in range(EXPERTS):
        back[i] = wide[2 * i : 2 * i + 2, :].astype(BF16)

    @pl.loop(1, EXPERTS)
    def _(k):
        to = (e + k) % EXPERTS
        pltpu.make_async_remote_copy(
            src_ref=back.at[to], dst_ref=ret.at[e], send_sem=back_send.at[0], recv_sem=back_recv.at[0],
            device_id=(c, to), device_id_type=MESH,
        ).start()

    ret[e] = back[e]

    all_of(back.at[pl.ds(0, EXPERTS - 1)], back_send.at[0], back_recv.at[0]).wait()

    all_of(tok.at[pl.ds(0, 31 * ROWS)], tok_send.at[0], tok_recv.at[0]).wait_send()
    all_of(kv.at[pl.ds(0, 26 * SEQ + 10 * SEQ // 2)], kv_send.at[0], kv_recv.at[0]).wait_send()
    for kind, blocks, columns in ((0, 31, MAIN), (1, 30, SIDE), (2, 16, 2 * SIDE)):
        sent = part.at[pl.ds(0, blocks * ROWS), pl.ds(0, columns)]
        all_of(sent, rs_send.at[kind], z_sem.at[0]).wait_send()


def on_device(
    lin_query,
    lin_key,
    lin_value,
    log_decay,
    lin_gain,
    moe_input,
    routes,
    route_weight,
    gate_weight,
    up_weight,
    down_weight,
    soft_query,
    soft_kv,
):
    vmem, any_ = pl.BlockSpec(memory_space=pltpu.VMEM), pl.BlockSpec(memory_space=pl.ANY)
    smem = pl.BlockSpec(memory_space=pltpu.SMEM)
    dma = pltpu.SemaphoreType.DMA
    ret, lin, soft = pl.pallas_call(
        kernel,
        out_shape=(
            jax.ShapeDtypeStruct((EXPERTS, CAP, D), BF16),
            jax.ShapeDtypeStruct((SEQ, HEADS * HEAD), BF16),
            jax.ShapeDtypeStruct((SEQ, HEADS * HEAD), BF16),
        ),
        in_specs=[smem, vmem, vmem, any_, any_, any_] + [vmem] * 6,
        out_specs=(vmem, vmem, vmem),
        scratch_shapes=[
            pltpu.VMEM((CTX * SEQ, 2 * HEAD), BF16),
            pltpu.VMEM((CTX * ROWS, D), BF16),
            pltpu.VMEM((CTX * ROWS, D), BF16),
            pltpu.VMEM((8 * ROWS, D), BF16),
            pltpu.VMEM((16 * ROWS, D), BF16),
            pltpu.VMEM((2 * ROWS, D), BF16),
            pltpu.VMEM((4 * ROWS, D), BF16),
            pltpu.VMEM((ROWS, MAIN), BF16),
            pltpu.VMEM((16 * ROWS, 2 * SIDE), BF16),
            pltpu.VMEM((EXPERTS, CAP, D), BF16),
            pltpu.VMEM((EXPERTS, CAP, D), BF16),
            pltpu.VMEM((EXPERTS, CAP, D), BF16),
            pltpu.VMEM((ROWS, D), F32),
            pltpu.VMEM((FF, D), BF16),
            pltpu.VMEM((FF, D), BF16),
            pltpu.VMEM((FF, D), BF16),
            pltpu.VMEM((CTX * ROWS, FF), BF16),
            pltpu.VMEM((SEQ, CTX * SEQ), F32),
            pltpu.VMEM((SEQ, HEADS), F32),
            pltpu.VMEM((HEADS, SEQ), F32),
            pltpu.VMEM((CTX, 48, HEAD), BF16),
            pltpu.VMEM((CTX, 48, HEAD), BF16),
            pltpu.VMEM((CTX, 32, HEAD), BF16),
            pltpu.VMEM((CTX, 32, HEAD), BF16),
            dma((3,)),
            dma((1,)), dma((2 * CTX + 1,)), dma((1,)), dma((CTX,)), dma((3,)),
            dma((16,)), dma((32,)), dma((4,)), dma((8,)), dma((17,)),
            dma((1,)), dma((1,)), dma((1,)), dma((1,)),
            dma((1,)), dma((1,)), dma((1,)), dma((1,)),
        ],
        compiler_params=pltpu.CompilerParams(
            collective_id=0, has_side_effects=True, vmem_limit_bytes=58 * 2**20
        ),
    )(
        routes.T,
        moe_input,
        soft_kv.reshape(SEQ, 2, HEAD),
        gate_weight.reshape(D, FF).T,
        up_weight.reshape(D, FF).T,
        down_weight.reshape(FF, D),
        lin_query,
        lin_key,
        lin_value,
        log_decay.T,
        lin_gain.reshape(1, HEADS * HEAD),
        soft_query,
    )
    lin_out, moe_out, soft_out = pl.pallas_call(
        finish,
        out_shape=(
            jax.ShapeDtypeStruct((SEQ, HEADS * HEAD), BF16),
            jax.ShapeDtypeStruct(moe_input.shape, BF16),
            jax.ShapeDtypeStruct((SEQ, HEADS * HEAD), BF16),
        ),
        in_specs=[smem, smem, vmem, vmem, vmem],
        out_specs=(vmem, vmem, vmem),
        scratch_shapes=[pltpu.VMEM((ROWS, D), F32)],
    )(routes.T, route_weight.T, ret, lin, soft)
    return (lin_out, moe_out, soft_out)


def solution(mesh):
    placed = (
        P("ctx", "exp"),
        P("ctx", "exp"),
        P("ctx", "exp"),
        P("ctx", "exp"),
        P("exp"),
        P(("ctx", "exp"), None),
        P(("ctx", "exp"), None),
        P(("ctx", "exp"), None),
        P("exp", None, "ctx"),
        P("exp", None, "ctx"),
        P("exp", "ctx", None),
        P("ctx", "exp"),
        P("ctx", "exp", None, None),
    )
    return jax.shard_map(
        on_device,
        mesh=mesh,
        in_specs=placed,
        out_specs=(P("ctx", "exp"), P(("ctx", "exp"), None), P("ctx", "exp")),
        check_vma=False,
    )
```
